128 devices in a mesh: gx: 16 (over z, x), gy: 8 (over y, core).
Axes of the slice: x: 4, y: 4, z: 4, core: 2. Of those that a mesh axis runs over, the one named last changes fastest.
Arguments:
- flow_field: float32 [1024, 4, 512], P(('gx', 'gy')), may hold values from -6 to 6
- enc_first: float32 [4, 128], replicated, may hold values from -3 to 3
- enc_second: bfloat16 [128, 128], replicated, may hold values from -0.5 to 0.5
- send_rows: int32 [128, 128, 8], P(('gx', 'gy')), may hold values from 0 to 512, as said below
- part_sizes: int32 [128, 128], P(('gx', 'gy')), may hold values from 0 to 8, as said below
- halo_rows: int32 [128, 2, 2, 64], P(('gx', 'gy')), may hold values from 0 to 1023, as said below
- neighbours: int32 [8, 131072], P(None, ('gx', 'gy')), may hold values from 0 to 1536, as said below
- edge_first: bfloat16 [2, 384, 128], replicated, may hold values from -0.3125 to 0.3125
- edge_second: bfloat16 [2, 128, 128], replicated, may hold values from -0.5 to 0.5
- node_first: bfloat16 [2, 256, 128], replicated, may hold values from -0.375 to 0.375
- node_second: bfloat16 [2, 128, 128], replicated, may hold values from -0.5 to 0.5
Outputs:
- node_latents: bfloat16 [131072, 128], P(('gx', 'gy'))
The draws below stay inside these ranges and needn't reach their ends.
Inputs may be any that keep to these rules, and one draw needn't show every extreme that they name: For every source s and target d, send_rows[s, d, k] is a node of s for k < part_sizes[d, s] and 512 for the other slots; every node of s stands exactly once in send_rows[s]. part_sizes[d, s] is the number of nodes that device s sends to device d; the sum over d is 512 for every s; in every draw some device d receives 8 nodes from every source. `halo_rows`: every entry is an occupied slot of the device's graph nodes (s*8+k with k < part_sizes[d, s]); entries may repeat. `neighbours`: each entry is 1537 - 1 (no edge), an occupied slot of the device's own graph nodes, or a received halo row 1024 .. 1535; empty slots have no edges; every occupied node has 4 to 8 edges in its first slots, and some node of every device has 8.
All inputs are finite; a program needn't handle non-finite values.
Results may differ from the reference program's by a relative error of at most 0.015.
Values may be sent and summed in bfloat16 or wider, within the bound.
A program may use at most 64 MiB of HBM per device.

```python
import jax
import jax.numpy as jnp
import numpy as np
from jax import lax

E_DEV = 8
CHANNELS = 4
LATENT = 128
MLP_HIDDEN = 128
DEGREE = 8
LAYERS = 2
ELEM_POINTS = 512
ELEM_NODES = 64
ELEMS = 1024
NODES_DEV = 512
CAP = 8
GCAP = 1024
HCAP = 64
EXT = 1537
N_GX = 16
N_GY = 8
DEVICES = 128


def plan_counts(key):
    hot_device = jax.random.randint(jax.random.fold_in(key, 501), (), 0, DEVICES)
    others = DEVICES - 1
    remaining = NODES_DEV - CAP
    base_count = remaining // others
    extra_count = remaining - base_count * others

    def shuffle_one(subkey):
        return jax.random.permutation(subkey, others)
    shuffled = jax.vmap(shuffle_one)(jax.random.split(jax.random.fold_in(key, 502), DEVICES))
    target = jnp.arange(DEVICES)
    position = jnp.clip(jnp.where(target < hot_device, target, target - 1), 0, others - 1)
    ranked = jnp.take(shuffled, position, axis=1)
    counts = base_count + (ranked < extra_count).astype(jnp.int32)
    counts = jnp.where(target[None, :] == hot_device, CAP, counts)
    return counts.astype(jnp.int32)


def table_layout(key):
    counts = plan_counts(key)
    incoming = counts.T
    slot_index = jnp.arange(CAP)
    occupied = (slot_index[None, None, :] < incoming[:, :, None]).reshape(DEVICES, GCAP)
    scores = (1 - occupied.astype(jnp.int32)) * GCAP + jnp.arange(GCAP)[None, :]
    ordering = jnp.argsort(scores, axis=1).astype(jnp.int32)
    filled = jnp.maximum(jnp.sum(occupied.astype(jnp.int32), axis=1), 1)
    return (occupied, ordering, filled)


def draw_send_rows(key, part):
    counts = plan_counts(key)
    key = jax.random.fold_in(key, 11)

    def shuffle_nodes(subkey):
        return jax.random.permutation(subkey, NODES_DEV)
    shuffled = jax.vmap(shuffle_nodes)(jax.random.split(key, DEVICES)).astype(jnp.int32)
    offsets = jnp.cumsum(counts, axis=1) - counts
    slot_index = jnp.arange(CAP)
    wanted = jnp.minimum(offsets[:, :, None] + slot_index[None, None, :], NODES_DEV - 1)
    picked = jnp.take_along_axis(shuffled, wanted.reshape(DEVICES, DEVICES * CAP), axis=1)
    picked = picked.reshape(DEVICES, DEVICES, CAP)
    return jnp.where(slot_index[None, None, :] < counts[:, :, None], picked, NODES_DEV).astype(jnp.int32)


def draw_part_sizes(key, part):
    counts = plan_counts(key)
    return counts.T.astype(jnp.int32)


def draw_halo_rows(key, part):
    occupied, ordering, filled = table_layout(key)
    key = jax.random.fold_in(key, 12)
    picked = jax.random.randint(key, (DEVICES, 4 * HCAP), 0, 2 ** 30) % filled[:, None]
    chosen = jnp.take_along_axis(ordering, picked, axis=1)
    return chosen.reshape(DEVICES, 2, 2, HCAP).astype(jnp.int32)


def draw_neighbours(key, part):
    occupied, ordering, filled = table_layout(key)
    key = jax.random.fold_in(key, 13)
    subkeys = jax.random.split(key, 4)
    degree = jax.random.randint(subkeys[0], (DEVICES, GCAP), 4, DEGREE + 1)
    first_node = ordering[:, 0]
    degree = jnp.where(jnp.arange(GCAP)[None, :] == first_node[:, None], DEGREE, degree)
    local_index = jax.random.randint(subkeys[1], (DEVICES, DEGREE * GCAP), 0, 2 ** 30) % filled[:, None]
    local_pick = jnp.take_along_axis(ordering, local_index, axis=1).reshape(DEVICES, DEGREE, GCAP)
    remote_pick = GCAP + jax.random.randint(subkeys[2], (DEVICES, DEGREE, GCAP), 0, 8 * HCAP)
    remote = jax.random.randint(subkeys[3], (DEVICES, DEGREE, GCAP), 0, 8) == 0
    target = jnp.where(remote, remote_pick, local_pick)
    alive_edge = (jnp.arange(DEGREE)[None, :, None] < degree[:, None, :]) & occupied[:, None, :]
    linked = jnp.where(alive_edge, target, EXT - 1)
    return linked.transpose(1, 0, 2).reshape(DEGREE, DEVICES * GCAP).astype(jnp.int32)


def shard_levels(rng, extent, cuts, least, largest):
    level = 1.0
    for axis_at, shards_of in cuts:
        heights = jax.random.uniform(jax.random.fold_in(jax.random.fold_in(rng, 6), axis_at), (shards_of,), jnp.float32, least / len(cuts), largest / len(cuts))
        level = level * jnp.repeat(jnp.exp(heights), extent[axis_at] // shards_of).reshape((-1,) + (1,) * (len(extent) - 1 - axis_at))
    return level


def scatter_about(own_key, extent, width, most, shards=(), kind=jnp.bfloat16):
    result = width * jax.random.normal(own_key, extent, jnp.float32)
    if shards:
        result = result * shard_levels(own_key, extent, shards, -0.22, 0.18)
    return jnp.clip(result, -most, most).astype(kind)


def setup_inputs(seed: int = 0) -> dict:
    arg_keys = jax.random.split(jax.random.key(seed), 12)
    flow_field = scatter_about(arg_keys[0], (ELEMS, CHANNELS, ELEM_POINTS), 1.0, 6.0, ((0, 128),), jnp.float32)
    enc_first = scatter_about(arg_keys[1], (CHANNELS, MLP_HIDDEN), CHANNELS ** -0.5, 3.0, (), jnp.float32)
    enc_second = scatter_about(arg_keys[2], (MLP_HIDDEN, LATENT), MLP_HIDDEN ** -0.5, 0.5)
    send_rows = draw_send_rows(jax.random.fold_in(arg_keys[11], 71), 0)
    part_sizes = draw_part_sizes(jax.random.fold_in(arg_keys[11], 71), 0)
    halo_rows = draw_halo_rows(jax.random.fold_in(arg_keys[11], 71), 0)
    neighbours = draw_neighbours(jax.random.fold_in(arg_keys[11], 71), 0)
    edge_first = scatter_about(arg_keys[7], (LAYERS, 3 * LATENT, MLP_HIDDEN), (3 * LATENT) ** -0.5, 0.3125)
    edge_second = scatter_about(arg_keys[8], (LAYERS, MLP_HIDDEN, LATENT), MLP_HIDDEN ** -0.5, 0.5)
    node_first = scatter_about(arg_keys[9], (LAYERS, 2 * LATENT, MLP_HIDDEN), (2 * LATENT) ** -0.5, 0.375)
    node_second = scatter_about(arg_keys[10], (LAYERS, MLP_HIDDEN, LATENT), MLP_HIDDEN ** -0.5, 0.5)
    return dict(flow_field=flow_field, enc_first=enc_first, enc_second=enc_second, send_rows=send_rows, part_sizes=part_sizes, halo_rows=halo_rows, neighbours=neighbours, edge_first=edge_first, edge_second=edge_second, node_first=node_first, node_second=node_second)


GLL_POINTS = (-1.0, -0.8717401485096066, -0.5917001814331423, -0.2092992179024789, 0.2092992179024789, 0.5917001814331423, 0.8717401485096066, 1.0)
EPS = 1e-05

def interp_table():
    gll_nodes = np.array(GLL_POINTS)
    targets = np.array([-0.75, -0.25, 0.25, 0.75])
    basis_line = np.ones((4, 8))
    for j in range(8):
        for m in range(8):
            if m != j:
                basis_line[:, j] *= (targets - gll_nodes[m]) / (gll_nodes[j] - gll_nodes[m])
    return np.kron(np.kron(basis_line, basis_line), basis_line).astype(np.float32)

def layer_norm(values):
    center = values - lax.optimization_barrier(jnp.mean(values, axis=-1, keepdims=True))
    spread = lax.optimization_barrier(jnp.mean(center * center, axis=-1, keepdims=True))
    return center * lax.rsqrt(spread + EPS)

def encode(graph_part, enc_first, enc_second):
    preact = jnp.einsum('cn,ch->nh', graph_part, enc_first, precision=lax.Precision.HIGHEST)
    hidden = jax.nn.silu(preact).astype(jnp.bfloat16)
    return layer_norm(jnp.dot(hidden, enc_second, preferred_element_type=jnp.float32)).astype(jnp.bfloat16)

def edge_pass(node_state, received, link_table, edge_prev, w_first, w_second):
    latent_width = node_state.shape[1]
    extended = jnp.concatenate([node_state, received.reshape(-1, latent_width), jnp.zeros((1, latent_width), node_state.dtype)], axis=0)
    src_term = jnp.dot(node_state, w_first[latent_width:2 * latent_width], preferred_element_type=jnp.float32)
    dst_term = jnp.dot(extended, w_first[2 * latent_width:], preferred_element_type=jnp.float32)
    preact = src_term[None, :, :] + jnp.take(dst_term, link_table, axis=0)
    if edge_prev is not None:
        own_term = jnp.dot(edge_prev.reshape(-1, latent_width), w_first[:latent_width], preferred_element_type=jnp.float32)
        preact = preact + own_term.reshape(preact.shape)
    hidden = jax.nn.silu(preact).astype(jnp.bfloat16)
    update = layer_norm(jnp.dot(hidden.reshape(-1, hidden.shape[2]), w_second, preferred_element_type=jnp.float32)).reshape(link_table.shape + (latent_width,))
    if edge_prev is not None:
        update = edge_prev.astype(jnp.float32) + update
    alive_edge = (link_table != extended.shape[0] - 1)[..., None]
    edge_new = jnp.where(alive_edge, update, jnp.zeros((), jnp.float32)).astype(jnp.bfloat16)
    summed = jnp.zeros((extended.shape[0], latent_width), jnp.float32).at[link_table.reshape(-1)].add(edge_new.reshape(-1, latent_width).astype(jnp.float32))
    return (edge_new, summed)

def node_pass(node_state, local_sum, occupied, w_first, w_second):
    latent_width = node_state.shape[-1]
    aggregate = local_sum.astype(jnp.bfloat16)
    preact = jnp.dot(node_state, w_first[:latent_width], preferred_element_type=jnp.float32)
    preact = preact + jnp.dot(aggregate, w_first[latent_width:], preferred_element_type=jnp.float32)
    hidden = jax.nn.silu(preact).astype(jnp.bfloat16)
    update = layer_norm(jnp.dot(hidden, w_second, preferred_element_type=jnp.float32))
    return jnp.where(occupied[:, None], node_state.astype(jnp.float32) + update, jnp.zeros((), jnp.float32)).astype(jnp.bfloat16)

def forward_blocks(sent):
    lower_x = jnp.roll(sent, 1, axis=0)
    upper_x = jnp.roll(sent, -1, axis=0)
    lower_y = jnp.roll(sent, 1, axis=1)
    upper_y = jnp.roll(sent, -1, axis=1)
    blocks = [lower_x[:, :, 1, 0], lower_x[:, :, 1, 1], upper_x[:, :, 0, 0], upper_x[:, :, 0, 1], lower_y[:, :, 0, 1], lower_y[:, :, 1, 1], upper_y[:, :, 0, 0], upper_y[:, :, 1, 0]]
    return jnp.stack(blocks, axis=2)

def backward_blocks(sums):
    lower_x = jnp.roll(sums, 1, axis=0)
    upper_x = jnp.roll(sums, -1, axis=0)
    lower_y = jnp.roll(sums, 1, axis=1)
    upper_y = jnp.roll(sums, -1, axis=1)
    first_row = jnp.stack([lower_x[:, :, 2] + lower_y[:, :, 6], lower_x[:, :, 3] + upper_y[:, :, 4]], axis=2)
    second_row = jnp.stack([upper_x[:, :, 0] + lower_y[:, :, 7], upper_x[:, :, 1] + upper_y[:, :, 5]], axis=2)
    return jnp.stack([first_row, second_row], axis=2)

def reference(flow_field, enc_first, enc_second, send_rows, part_sizes, halo_rows, neighbours, edge_first, edge_second, node_first, node_second):
    interp = jnp.asarray(interp_table())
    sampled = jnp.dot(flow_field.reshape(ELEMS * CHANNELS, ELEM_POINTS), interp.T, precision=lax.Precision.HIGHEST)
    columns = sampled.reshape(DEVICES, E_DEV, CHANNELS, ELEM_NODES).transpose(0, 2, 1, 3).reshape(DEVICES, CHANNELS, NODES_DEV)
    padded_columns = jnp.concatenate([columns, jnp.zeros((DEVICES, CHANNELS, 1), columns.dtype)], axis=2)

    def pick_source(source_columns, source_slots):
        return jnp.take(source_columns, source_slots, axis=1)
    moved = jax.vmap(pick_source)(padded_columns, send_rows)
    graph_columns = moved.transpose(2, 1, 0, 3).reshape(DEVICES, CHANNELS, GCAP)
    occupied = (jnp.arange(CAP)[None, None, :] < part_sizes[:, :, None]).reshape(DEVICES, GCAP)

    def encode_one(graph_part):
        return encode(graph_part, enc_first, enc_second)
    latent = jax.vmap(encode_one)(graph_columns)
    node_state = jnp.where(occupied[..., None], latent, jnp.zeros((), jnp.bfloat16))
    link_table = neighbours.reshape(DEGREE, DEVICES, GCAP).transpose(1, 0, 2)

    def take_halo(device_state, device_ids):
        return jnp.take(device_state, device_ids, axis=0)

    def add_back(device_sum, device_ids, device_extra):
        return device_sum.at[device_ids].add(device_extra)
    states = [node_state]
    receives = []
    for layer_index in range(LAYERS):
        sent = jax.vmap(take_halo)(node_state, halo_rows)
        received = forward_blocks(sent.reshape(N_GX, N_GY, 2, 2, HCAP, LATENT)).reshape(DEVICES, 8, HCAP, LATENT)
        receives.append(received)

        def device_pass(inputs):
            device_links, past_states, past_receives = inputs
            edge_state = None
            summed = None
            for past_layer in range(len(past_states)):
                edge_state, summed = edge_pass(past_states[past_layer], past_receives[past_layer], device_links, edge_state, edge_first[past_layer], edge_second[past_layer])
            return summed
        summed = lax.map(device_pass, (link_table, tuple(states), tuple(receives)))
        halo_sums = summed[:, GCAP:GCAP + 8 * HCAP].reshape(N_GX, N_GY, 8, HCAP, LATENT)
        returned = backward_blocks(halo_sums).reshape(DEVICES, 4 * HCAP, LATENT)
        local_sum = jax.vmap(add_back)(summed[:, :GCAP], halo_rows.reshape(DEVICES, 4 * HCAP), returned)
        node_state = node_pass(node_state.reshape(DEVICES * GCAP, LATENT), local_sum.reshape(DEVICES * GCAP, LATENT), occupied.reshape(-1), node_first[layer_index], node_second[layer_index]).reshape(DEVICES, GCAP, LATENT)
        states.append(node_state)
    return node_state.reshape(DEVICES * GCAP, LATENT)
```

```python
import functools

import jax
import jax.numpy as jnp
import numpy as np
from jax import lax
from jax.experimental import pallas as pl
from jax.experimental.pallas import tpu as pltpu
from jax.sharding import PartitionSpec as P

MESH = pl.DeviceIdType.MESH
F32 = jnp.float32
BF16 = jnp.bfloat16
F8 = jnp.float8_e4m3fn

LAYERS = 2
GLL_POINTS = (
    -1.0,
    -0.8717401485096066,
    -0.5917001814331423,
    -0.2092992179024789,
    0.2092992179024789,
    0.5917001814331423,
    0.8717401485096066,
    1.0,
)
EPS = 1e-05
D = 128
NODES = 1024
HALO = 512
ROWS = NODES + HALO
SLOTS = 8
EDGES = SLOTS * NODES
CH = 512
STEPS = EDGES // CH
HALF = NODES // CH


def interp_table():
    gll_nodes = np.array(GLL_POINTS)
    targets = np.array([-0.75, -0.25, 0.25, 0.75])
    basis_line = np.ones((4, 8))
    for j in range(8):
        for m in range(8):
            if m != j:
                basis_line[:, j] *= (targets - gll_nodes[m]) / (gll_nodes[j] - gll_nodes[m])
    return np.kron(np.kron(basis_line, basis_line), basis_line).astype(np.float32)


def interp_parts():
    table = interp_table()
    high = table.astype(BF16)
    low = (table - high.astype(np.float32)).astype(BF16)
    return np.concatenate([high, low], axis=0)


def mm(a, b):
    return jnp.dot(a, b, preferred_element_type=F32)


def mm_t(a, b):
    return lax.dot_general(a, b, (((1,), (1,)), ((), ())), preferred_element_type=F32)


def two_terms(x, dtype):
    high = x.astype(dtype)
    return high, (x - high.astype(F32)).astype(dtype)


def half_silu(u):
    return u + u * jnp.tanh(u)


def norm_columns(v):
    spread = jnp.sum(v * v, axis=0, keepdims=True) * (1.0 / D)
    return v * lax.rsqrt(spread + EPS)


def centred_t(w):
    w = w.astype(F32)
    return (w - jnp.mean(w, axis=1, keepdims=True)).T.astype(BF16)


def scaled_t(w, scale):
    return (w.astype(F32).T * scale).astype(BF16)


def kernel(
    nx,
    ny,
    flow,
    interp,
    enc_first,
    enc_second,
    send_rows,
    halo,
    links,
    edge_first,
    edge_second,
    node_first,
    node_second,
    out,
    oht,
    e8,
    e16,
    part,
    t8,
    ohh,
    xs,
    wsrc,
    wown,
    wdst,
    we2,
    wn1,
    wn2,
    wenc1,
    wenc2,
    src,
    sbuf,
    r1,
    r2,
    hsend,
    hrecv,
    bsend,
    brecv,
    s1,
    q1,
    s2,
    q2,
    fs,
    fq,
    bs,
    bq,
):
    gx, gy = lax.axis_index("gx"), lax.axis_index("gy")

    def at_x(step):
        return (lax.rem(gx + (step + nx), nx), gy)

    def at_y(step):
        return (gx, lax.rem(gy + (step + ny), ny))

    barrier = pltpu.get_barrier_semaphore()
    for step in range(1, ny):
        pl.semaphore_signal(barrier, inc=1, device_id=at_y(step), device_id_type=MESH)
    for step in range(1, nx):
        pl.semaphore_signal(barrier, inc=1, device_id=at_x(step), device_id_type=MESH)

    tiles = []
    for e in range(8):
        f = flow[e]
        f = jnp.concatenate([f, f], axis=0)
        tiles.append(jnp.concatenate([f, f, f, f], axis=0))
    flow_high, flow_low = two_terms(jnp.concatenate(tiles, axis=0), BF16)
    main = mm_t(interp[...], flow_high)
    sampled = main[:64] + main[64:] + mm_t(interp[0:64, :], flow_low)
    columns = jnp.concatenate([sampled[:, 32 * e : 32 * e + 32] for e in range(8)], axis=0)
    col_high, col_low = two_terms(columns, BF16)
    table = jnp.concatenate(
        [
            col_high,
            jnp.ones((512, 8), BF16),
            jnp.zeros((512, 88), BF16),
            col_low,
            jnp.zeros((512, 96), BF16),
        ],
        axis=1,
    )
    lane = lax.broadcasted_iota(jnp.int32, (D, D), 1)
    picked = jnp.zeros((D, D), F32)
    slots = jnp.concatenate(
        [send_rows[0, pl.ds(y, nx, stride=ny), :] for y in range(ny)], axis=0
    )
    node_ids = lax.broadcasted_iota(jnp.int32, (D, 512), 1)
    for k in range(SLOTS):
        choose = (slots[:, k : k + 1] == node_ids).astype(F32).astype(BF16)
        both = mm(choose, table)
        mine = ((lane < 32) & (lane // 4 == k)) | (lane == 32 + k)
        picked = picked + jnp.where(mine, both[:, :D] + both[:, D:], 0.0)
    for y in range(ny):
        for x in range(nx):
            row = y * nx + x
            sbuf[y, x] = picked[row : row + 1, :]

    pl.semaphore_wait(barrier, nx + ny - 2)

    first = []
    for step in range(1, ny):
        target = at_y(step)
        copy = pltpu.make_async_remote_copy(
            src_ref=sbuf.at[target[1]],
            dst_ref=r1.at[:, gy],
            send_sem=s1.at[step - 1],
            recv_sem=q1.at[step - 1],
            device_id=target,
            device_id_type=MESH,
        )
        copy.start()
        first.append(copy)
    r1[:, gy] = sbuf[gy]

    sub8 = lax.broadcasted_iota(jnp.int32, (D, CH), 0).astype(jnp.int8)

    def make_oht(c, carry):
        k, half = c // HALF, lax.rem(c, HALF)
        ids = links[pl.ds(k, 1), pl.ds(pl.multiple_of(half * CH, CH), CH)]
        where = pl.ds(pl.multiple_of(c * CH, CH), CH)
        for a in range(ROWS // D):
            key = ids - D * a
            key = jnp.where((key >= 0) & (key < D), key, -1).astype(jnp.int8)
            oht[pl.ds(a * D, D), where] = jnp.where(
                key == sub8, jnp.ones((), F8), jnp.zeros((), F8)
            )
        return carry

    lax.fori_loop(0, STEPS // 2, make_oht, 0)

    for copy in first:
        copy.wait_recv()
    second = []
    for step in range(1, nx):
        target = at_x(step)
        copy = pltpu.make_async_remote_copy(
            src_ref=r1.at[target[0]],
            dst_ref=r2.at[gx],
            send_sem=s2.at[step - 1],
            recv_sem=q2.at[step - 1],
            device_id=target,
            device_id_type=MESH,
        )
        copy.start()
        second.append(copy)
    r2[gx] = r1[gx]

    lax.fori_loop(STEPS // 2, STEPS, make_oht, 0)

    spread_first = jnp.concatenate([enc_first[...], enc_first[...]], axis=0)
    spread_first = jnp.concatenate([spread_first] * 16, axis=0).T
    enc_high, enc_low = two_terms(jnp.where(lane < 32, spread_first * 0.5, 0.0), BF16)
    wenc1[0:D, 0:D] = enc_high
    wenc1[0:D, D : 2 * D] = enc_high
    wenc1[D : 2 * D, 0:D] = enc_low
    wenc1[D : 2 * D, D : 2 * D] = jnp.zeros((D, D), BF16)
    mark = lax.broadcasted_iota(jnp.int32, (16, 2 * D), 1)
    wenc1[2 * D : 2 * D + 16, :] = ((mark >= 32) & (mark < 40)).astype(F32).astype(BF16)
    wenc2[...] = centred_t(enc_second[...])
    for l in range(LAYERS):
        wown[l] = scaled_t(edge_first[l, 0:D, :], 4.0)
        wsrc[l] = scaled_t(edge_first[l, D : 2 * D, :], 4.0)
        wdst[l] = scaled_t(edge_first[l, 2 * D : 3 * D, :], 4.0)
        we2[l] = centred_t(edge_second[l])
        wn1[l, :, 0:D] = scaled_t(node_first[l, 0:D, :], 0.5)
        wn1[l, :, D : 2 * D] = scaled_t(node_first[l, D : 2 * D, :], 0.5)
        wn2[l] = centred_t(node_second[l])

    node_rows = lax.broadcasted_iota(jnp.int32, (NODES, D), 0)
    for j, (p, q) in enumerate((((1, 0), (1, 1)), ((0, 0), (0, 1)), ((0, 1), (1, 1)), ((0, 0), (1, 0)))):
        ids = jnp.concatenate([halo[0, p[0], p[1] : p[1] + 1, :], halo[0, q[0], q[1] : q[1] + 1, :]], axis=1)
        ohh[:, D * j : D * j + D] = (ids == node_rows).astype(F32).astype(BF16)

    for copy in first:
        copy.wait_send()
    for copy in second:
        copy.wait_recv()

    sub = lax.broadcasted_iota(jnp.int32, (8, D), 0)
    lane8 = lax.broadcasted_iota(jnp.int32, (8, D), 1)
    keep = ((lane8 < 32) & (lane8 // 4 == sub)) | (lane8 == 32 + sub)
    for x in range(nx):
        for y in range(0, ny, 2):
            rows = jnp.concatenate(
                [
                    jnp.where(keep, jnp.broadcast_to(r2[x, y], (8, D)), 0.0),
                    jnp.where(keep, jnp.broadcast_to(r2[x, y + 1], (8, D)), 0.0),
                ],
                axis=0,
            )
            high, low = two_terms(rows, BF16)
            base = (x * ny + y) * 8
            xs[base : base + 16, 0:D] = high
            xs[base : base + 16, D : 2 * D] = low
    pre = mm_t(wenc1[...], xs[...])
    filled = pre[2 * D : 2 * D + 1, :] > 0.5
    hidden = half_silu(pre[:D] + pre[D : 2 * D]).astype(BF16)
    h = norm_columns(mm(wenc2[...], hidden))
    h = jnp.where(filled, h, 0.0).astype(BF16)
    for copy in second:
        copy.wait_send()

    forward = (at_x(1), at_x(-1), at_y(1), at_y(-1))
    backward = (at_x(-1), at_x(1), at_y(-1), at_y(1))

    for l in range(LAYERS):
        proj = mm(wdst[l], h)
        border = mm(proj.astype(BF16), ohh[...]).astype(BF16)
        copies = []
        for j in range(4):
            hsend[l, j] = border[:, D * j : D * j + D]
            copy = pltpu.make_async_remote_copy(
                src_ref=hsend.at[l, j],
                dst_ref=hrecv.at[l, j],
                send_sem=fs.at[l, j],
                recv_sem=fq.at[l, j],
                device_id=forward[j],
                device_id_type=MESH,
            )
            copy.start()
            copies.append(copy)
        high, low = two_terms(proj, F8)
        t8[0:D, 0:NODES] = high
        t8[D : 2 * D, 0:NODES] = low
        src[...] = mm(wsrc[l], h)

        def local_step(c, carry):
            half = lax.rem(c, HALF)
            where = pl.ds(pl.multiple_of(c * CH, CH), CH)
            got = mm(t8[:, 0:NODES], oht[0:NODES, where])
            u = got[:D] + got[D:] + src[:, pl.ds(pl.multiple_of(half * CH, CH), CH)]
            if l > 0:
                u = u + mm(wown[l], e16[:, where])
            part[c] = u
            return carry

        lax.fori_loop(0, STEPS, local_step, 0)

        for j, copy in enumerate(copies):
            copy.wait_recv()
            high, low = two_terms(hrecv[l, j].astype(F32), F8)
            t8[0:D, NODES + D * j : NODES + D * j + D] = high
            t8[D : 2 * D, NODES + D * j : NODES + D * j + D] = low

        def edge_step(c, carry):
            where = pl.ds(pl.multiple_of(c * CH, CH), CH)
            got = mm(t8[:, NODES:ROWS], oht[NODES:ROWS, where])
            u = (part[c] + got[:D] + got[D:]) * 0.125
            new = norm_columns(mm(we2[l], half_silu(u).astype(BF16)))
            if l > 0:
                new = new + e16[:, where].astype(F32)
            if l + 1 < LAYERS:
                e16[:, where] = new.astype(BF16)
            high, low = two_terms(new * 16.0, F8)
            e8[0:D, where] = high
            e8[D : 2 * D, where] = low
            return carry

        lax.fori_loop(0, STEPS, edge_step, 0)

        sums = mm_t(e8[...], oht[NODES:ROWS, :])
        sums = ((sums[:D] + sums[D:]) * 0.0625).astype(BF16)
        back = []
        for j in range(4):
            bsend[l, j] = sums[:, D * j : D * j + D]
            copy = pltpu.make_async_remote_copy(
                src_ref=bsend.at[l, j],
                dst_ref=brecv.at[l, j],
                send_sem=bs.at[l, j],
                recv_sem=bq.at[l, j],
                device_id=backward[j],
                device_id_type=MESH,
            )
            copy.start()
            back.append(copy)
        sums = mm_t(e8[...], oht[0:NODES, :])
        sums = (sums[:D] + sums[D:]) * 0.0625
        for copy in back:
            copy.wait_recv()
        returned = jnp.concatenate([brecv[l, j] for j in range(4)], axis=1)
        sums = sums + mm_t(returned, ohh[...])
        pre = mm(wn1[l], jnp.concatenate([h, sums.astype(BF16)], axis=0))
        new = h.astype(F32) + norm_columns(mm(wn2[l], half_silu(pre).astype(BF16)))
        new = jnp.where(filled, new, 0.0)
        for copy in copies:
            copy.wait_send()
        for copy in back:
            copy.wait_send()
        if l + 1 < LAYERS:
            h = new.astype(BF16)
        else:
            out[...] = new.T.astype(BF16)


def solution(mesh):
    nx, ny = mesh.shape["gx"], mesh.shape["gy"]

    def shards(
        flow_field,
        enc_first,
        enc_second,
        send_rows,
        part_sizes,
        halo_rows,
        neighbours,
        edge_first,
        edge_second,
        node_first,
        node_second,
    ):
        del part_sizes
        vmem = pl.BlockSpec(memory_space=pltpu.VMEM)
        dma = pltpu.SemaphoreType.DMA
        return pl.pallas_call(
            functools.partial(kernel, nx, ny),
            out_shape=jax.ShapeDtypeStruct((NODES, D), BF16),
            in_specs=[vmem] * 11,
            out_specs=vmem,
            scratch_shapes=[
                pltpu.VMEM((ROWS, EDGES), F8),
                pltpu.VMEM((2 * D, EDGES), F8),
                pltpu.VMEM((D, EDGES), BF16),
                pltpu.VMEM((STEPS, D, CH), F32),
                pltpu.VMEM((2 * D, ROWS), F8),
                pltpu.VMEM((NODES, HALO), BF16),
                pltpu.VMEM((NODES, 2 * D), BF16),
                pltpu.VMEM((LAYERS, D, D), BF16),
                pltpu.VMEM((LAYERS, D, D), BF16),
                pltpu.VMEM((LAYERS, D, D), BF16),
                pltpu.VMEM((LAYERS, D, D), BF16),
                pltpu.VMEM((LAYERS, D, 2 * D), BF16),
                pltpu.VMEM((LAYERS, D, D), BF16),
                pltpu.VMEM((2 * D + 16, 2 * D), BF16),
                pltpu.VMEM((D, D), BF16),
                pltpu.VMEM((D, NODES), F32),
                pltpu.VMEM((ny, nx, 1, D), F32),
                pltpu.VMEM((nx, ny, 1, D), F32),
                pltpu.VMEM((nx, ny, 1, D), F32),
                pltpu.VMEM((LAYERS, 4, D, D), BF16),
                pltpu.VMEM((LAYERS, 4, D, D), BF16),
                pltpu.VMEM((LAYERS, 4, D, D), BF16),
                pltpu.VMEM((LAYERS, 4, D, D), BF16),
                dma((ny - 1,)),
                dma((ny - 1,)),
                dma((nx - 1,)),
                dma((nx - 1,)),
                dma((LAYERS, 4)),
                dma((LAYERS, 4)),
                dma((LAYERS, 4)),
                dma((LAYERS, 4)),
            ],
            compiler_params=pltpu.CompilerParams(
                collective_id=0, has_side_effects=True, vmem_limit_bytes=48 << 20
            ),
        )(
            flow_field,
            jnp.asarray(interp_parts()),
            enc_first,
            enc_second,
            send_rows,
            halo_rows,
            neighbours,
            edge_first,
            edge_second,
            node_first,
            node_second,
        )

    in_specs = (
        P(("gx", "gy"), None, None),
        P(),
        P(),
        P(("gx", "gy"), None, None),
        P(("gx", "gy"), None),
        P(("gx", "gy"), None, None, None),
        P(None, ("gx", "gy")),
        P(),
        P(),
        P(),
        P(),
    )
    out_specs = P(("gx", "gy"), None)
    return jax.shard_map(shards, mesh=mesh, in_specs=in_specs, out_specs=out_specs, check_vma=False)
```

```python
import functools

import jax
import jax.numpy as jnp
import numpy as np
from jax import lax
from jax.experimental import pallas as pl
from jax.experimental.pallas import tpu as pltpu
from jax.sharding import PartitionSpec as P

MESH = pl.DeviceIdType.MESH
F32 = jnp.float32
BF16 = jnp.bfloat16
F8 = jnp.float8_e4m3fn

LAYERS = 2
GLL_POINTS = (
    -1.0,
    -0.8717401485096066,
    -0.5917001814331423,
    -0.2092992179024789,
    0.2092992179024789,
    0.5917001814331423,
    0.8717401485096066,
    1.0,
)
EPS = 1e-05
D = 128
NODES = 1024
HALO = 512
ROWS = NODES + HALO
SLOTS = 8
EDGES = SLOTS * NODES
GROUP = 4
CH = GROUP * NODES
STEPS = SLOTS // GROUP


def interp_table():
    gll_nodes = np.array(GLL_POINTS)
    targets = np.array([-0.75, -0.25, 0.25, 0.75])
    basis_line = np.ones((4, 8))
    for j in range(8):
        for m in range(8):
            if m != j:
                basis_line[:, j] *= (targets - gll_nodes[m]) / (gll_nodes[j] - gll_nodes[m])
    return np.kron(np.kron(basis_line, basis_line), basis_line).astype(np.float32)


def interp_parts():
    table = interp_table()
    high = table.astype(BF16)
    low = (table - high.astype(np.float32)).astype(BF16)
    return np.concatenate([high, low], axis=0)


def mm(a, b):
    return jnp.dot(a, b, preferred_element_type=F32)


def mm_t(a, b):
    return lax.dot_general(a, b, (((1,), (1,)), ((), ())), preferred_element_type=F32)


def two_terms(x, dtype):
    high = x.astype(dtype)
    return high, (x - high.astype(F32)).astype(dtype)


def half_silu(u):
    return u + u * jnp.tanh(u)


def norm_columns(v, scale=1.0):
    spread = jnp.sum(v * v, axis=0, keepdims=True) * (1.0 / D)
    return v * (lax.rsqrt(spread + EPS) * scale)


def centred_t(w):
    w = w.astype(F32)
    return (w - jnp.mean(w, axis=1, keepdims=True)).T.astype(BF16)


def scaled_t(w, scale):
    return (w.astype(F32).T * scale).astype(BF16)


def kernel(
    nx,
    ny,
    flow_hbm,
    interp_hbm,
    send_hbm,
    links_hbm,
    halo_hbm,
    enc_first_hbm,
    enc_second_hbm,
    edge_first_hbm,
    edge_second_hbm,
    node_first_hbm,
    node_second_hbm,
    out,
    flow,
    interp,
    send_rows,
    links,
    halo,
    enc_first,
    enc_second,
    edge_first,
    edge_second,
    node_first,
    node_second,
    oht,
    e8,
    e16,
    part,
    t8,
    ohh,
    xs,
    wsrc,
    wown,
    wdst,
    we2,
    wn1,
    wn2,
    wenc1,
    wenc2,
    src,
    ordered,
    sbuf,
    r1,
    mid,
    r2,
    hsend,
    hrecv,
    bsend,
    brecv,
    loads,
    s1,
    q1,
    s2,
    q2,
    fs,
    fq,
    bs,
    bq,
):
    gx, gy = lax.axis_index("gx"), lax.axis_index("gy")

    def at_x(step):
        return (lax.rem(gx + (step + nx), nx), gy)

    def at_y(step):
        return (gx, lax.rem(gy + (step + ny), ny))

    barrier = pltpu.get_barrier_semaphore()
    for step in range(1, ny):
        pl.semaphore_signal(barrier, inc=1, device_id=at_y(step), device_id_type=MESH)
    for step in range(1, nx):
        pl.semaphore_signal(barrier, inc=1, device_id=at_x(step), device_id_type=MESH)

    pairs = (
        (flow_hbm, flow),
        (interp_hbm, interp),
        (send_hbm, send_rows),
        (links_hbm, links),
        (halo_hbm, halo),
        (enc_first_hbm, enc_first),
        (enc_second_hbm, enc_second),
        (edge_first_hbm, edge_first),
        (edge_second_hbm, edge_second),
        (node_first_hbm, node_first),
        (node_second_hbm, node_second),
    )
    loading = [
        pltpu.make_async_copy(there, here, loads.at[i]) for i, (there, here) in enumerate(pairs)
    ]
    for copy in loading:
        copy.start()
    for copy in loading[:3]:
        copy.wait()

    tiles = []
    for e in range(8):
        f = flow[e]
        f = jnp.concatenate([f, f], axis=0)
        tiles.append(jnp.concatenate([f, f, f, f], axis=0))
    flow_high, flow_low = two_terms(jnp.concatenate(tiles, axis=0), BF16)
    main = mm_t(interp[...], flow_high)
    sampled = main[:64] + main[64:] + mm_t(interp[0:64, :], flow_low)
    columns = jnp.concatenate([sampled[:, 32 * e : 32 * e + 32] for e in range(8)], axis=0)
    col_high, col_low = two_terms(columns, BF16)
    table = jnp.concatenate(
        [
            col_high,
            jnp.ones((512, 8), BF16),
            jnp.zeros((512, 88), BF16),
            col_low,
            jnp.zeros((512, 96), BF16),
        ],
        axis=1,
    )
    lane = lax.broadcasted_iota(jnp.int32, (D, D), 1)
    picked = jnp.zeros((D, D), F32)
    ordered[...] = jnp.concatenate([send_rows[0]] * 16, axis=0).T
    slots = jnp.concatenate(
        [ordered[pl.ds(y, nx, stride=ny), :] for y in range(ny)], axis=0
    )
    node_ids = lax.broadcasted_iota(jnp.int32, (D, 512), 1)
    for k in range(SLOTS):
        choose = (slots[:, k : k + 1] == node_ids).astype(F32).astype(BF16)
        both = mm(choose, table)
        mine = ((lane < 32) & (lane // 4 == k)) | (lane == 32 + k)
        picked = picked + jnp.where(mine, both[:, :D] + both[:, D:], 0.0)
    for y in range(ny):
        sbuf[y] = picked[y * nx : y * nx + nx, :]

    pl.semaphore_wait(barrier, nx + ny - 2)

    first = []
    for step in range(1, ny):
        target = at_y(step)
        copy = pltpu.make_async_remote_copy(
            src_ref=sbuf.at[target[1]],
            dst_ref=r1.at[gy],
            send_sem=s1.at[step - 1],
            recv_sem=q1.at[step - 1],
            device_id=target,
            device_id_type=MESH,
        )
        copy.start()
        first.append(copy)
    r1[gy] = sbuf[gy]
    for copy in loading[3:]:
        copy.wait()

    sub8 = lax.broadcasted_iota(jnp.int32, (D, NODES), 0).astype(jnp.int8)

    def make_oht(k, carry):
        ids = links[pl.ds(k, 1), :]
        where = pl.ds(pl.multiple_of(k * NODES, NODES), NODES)
        for a in range(ROWS // D):
            key = ids - D * a
            key = jnp.where((key >= 0) & (key < D), key, -1).astype(jnp.int8)
            oht[pl.ds(a * D, D), where] = jnp.where(
                key == sub8, jnp.full((), 0.125, F8), jnp.zeros((), F8)
            )
        return carry

    lax.fori_loop(0, SLOTS // 2, make_oht, 0)

    for copy in first:
        copy.wait_recv()
    for x in range(nx):
        mid[x] = r1[:, x, :]
    second = []
    for step in range(1, nx):
        target = at_x(step)
        copy = pltpu.make_async_remote_copy(
            src_ref=mid.at[target[0]],
            dst_ref=r2.at[gx],
            send_sem=s2.at[step - 1],
            recv_sem=q2.at[step - 1],
            device_id=target,
            device_id_type=MESH,
        )
        copy.start()
        second.append(copy)
    r2[gx] = mid[gx]

    lax.fori_loop(SLOTS // 2, SLOTS, make_oht, 0)

    spread_first = jnp.concatenate([enc_first[...], enc_first[...]], axis=0)
    spread_first = jnp.concatenate([spread_first] * 16, axis=0).T
    enc_high, enc_low = two_terms(jnp.where(lane < 32, spread_first * 0.5, 0.0), BF16)
    wenc1[0:D, 0:D] = enc_high
    wenc1[0:D, D : 2 * D] = enc_high
    wenc1[D : 2 * D, 0:D] = enc_low
    wenc1[D : 2 * D, D : 2 * D] = jnp.zeros((D, D), BF16)
    mark = lax.broadcasted_iota(jnp.int32, (16, 2 * D), 1)
    wenc1[2 * D : 2 * D + 16, :] = ((mark >= 32) & (mark < 40)).astype(F32).astype(BF16)
    wenc2[...] = centred_t(enc_second[...])
    for l in range(LAYERS):
        wown[l] = scaled_t(edge_first[l, 0:D, :], 0.03125)
        wsrc[l] = scaled_t(edge_first[l, D : 2 * D, :], 0.5)
        wdst[l] = scaled_t(edge_first[l, 2 * D : 3 * D, :], 4.0)
        we2[l] = centred_t(edge_second[l])
        wn1[l, :, 0:D] = scaled_t(node_first[l, 0:D, :], 0.5)
        wn1[l, :, D : 2 * D] = scaled_t(node_first[l, D : 2 * D, :], 0.5)
        wn2[l] = centred_t(node_second[l])

    node_rows = lax.broadcasted_iota(jnp.int32, (NODES, D), 0)
    for j, (p, q) in enumerate((((1, 0), (1, 1)), ((0, 0), (0, 1)), ((0, 1), (1, 1)), ((0, 0), (1, 0)))):
        ids = jnp.concatenate([halo[0, p[0], p[1] : p[1] + 1, :], halo[0, q[0], q[1] : q[1] + 1, :]], axis=1)
        ohh[:, D * j : D * j + D] = (ids == node_rows).astype(F32).astype(BF16)

    for copy in first:
        copy.wait_send()
    for copy in second:
        copy.wait_recv()

    sub = lax.broadcasted_iota(jnp.int32, (8, D), 0)
    lane8 = lax.broadcasted_iota(jnp.int32, (8, D), 1)
    keep = ((lane8 < 32) & (lane8 // 4 == sub)) | (lane8 == 32 + sub)
    for x in range(nx):
        for y in range(0, ny, 2):
            rows = jnp.concatenate(
                [
                    jnp.where(keep, jnp.broadcast_to(r2[x, y : y + 1, :], (8, D)), 0.0),
                    jnp.where(keep, jnp.broadcast_to(r2[x, y + 1 : y + 2, :], (8, D)), 0.0),
                ],
                axis=0,
            )
            high, low = two_terms(rows, BF16)
            base = (x * ny + y) * 8
            xs[base : base + 16, 0:D] = high
            xs[base : base + 16, D : 2 * D] = low
    pre = mm_t(wenc1[...], xs[...])
    filled = pre[2 * D : 2 * D + 1, :] > 0.5
    hidden = half_silu(pre[:D] + pre[D : 2 * D]).astype(BF16)
    h = norm_columns(mm(wenc2[...], hidden))
    h = jnp.where(filled, h, 0.0).astype(BF16)
    for copy in second:
        copy.wait_send()

    forward = (at_x(1), at_x(-1), at_y(1), at_y(-1))
    backward = (at_x(-1), at_x(1), at_y(-1), at_y(1))

    for l in range(LAYERS):
        proj = mm(wdst[l], h)
        border = mm(proj.astype(BF16), ohh[...]).astype(BF16)
        copies = []
        for j in range(4):
            hsend[l, j] = border[:, D * j : D * j + D]
            copy = pltpu.make_async_remote_copy(
                src_ref=hsend.at[l, j],
                dst_ref=hrecv.at[l, j],
                send_sem=fs.at[l, j],
                recv_sem=fq.at[l, j],
                device_id=forward[j],
                device_id_type=MESH,
            )
            copy.start()
            copies.append(copy)
        high, low = two_terms(proj, F8)
        t8[0:D, 0:NODES] = high
        t8[D : 2 * D, 0:NODES] = low
        src[...] = mm(wsrc[l], h)

        def local_step(c, carry):
            where = pl.ds(pl.multiple_of(c * CH, CH), CH)
            got = mm(t8[:, 0:NODES], oht[0:NODES, where])
            u = got[:D] + got[D:] + jnp.concatenate([src[...]] * GROUP, axis=1)
            if l > 0:
                u = u + mm(wown[l], e16[:, where])
            part[c] = u
            return carry

        lax.fori_loop(0, STEPS, local_step, 0, unroll=2)

        for j, copy in enumerate(copies):
            copy.wait_recv()
            high, low = two_terms(hrecv[l, j].astype(F32), F8)
            t8[0:D, NODES + D * j : NODES + D * j + D] = high
            t8[D : 2 * D, NODES + D * j : NODES + D * j + D] = low

        def edge_step(c, carry):
            where = pl.ds(pl.multiple_of(c * CH, CH), CH)
            got = mm(t8[:, NODES:ROWS], oht[NODES:ROWS, where])
            u = (part[c] + got[:D] + got[D:]).astype(BF16)
            new = norm_columns(mm(we2[l], half_silu(u)), 16.0).astype(BF16)
            if l > 0:
                new = new + e16[:, where]
            if l + 1 < LAYERS:
                e16[:, where] = new
            high = new.astype(F8)
            e8[0:D, where] = high
            e8[D : 2 * D, where] = (new - high.astype(BF16)).astype(F8)
            return carry

        lax.fori_loop(0, STEPS, edge_step, 0, unroll=2)

        sums = mm_t(e8[...], oht[NODES:ROWS, :])
        sums = ((sums[:D] + sums[D:]) * 0.5).astype(BF16)
        back = []
        for j in range(4):
            bsend[l, j] = sums[:, D * j : D * j + D]
            copy = pltpu.make_async_remote_copy(
                src_ref=bsend.at[l, j],
                dst_ref=brecv.at[l, j],
                send_sem=bs.at[l, j],
                recv_sem=bq.at[l, j],
                device_id=backward[j],
                device_id_type=MESH,
            )
            copy.start()
            back.append(copy)
        sums = mm_t(e8[...], oht[0:NODES, :])
        sums = (sums[:D] + sums[D:]) * 0.5
        for copy in back:
            copy.wait_recv()
        returned = jnp.concatenate([brecv[l, j] for j in range(4)], axis=1)
        sums = sums + mm_t(returned, ohh[...])
        pre = mm(wn1[l], jnp.concatenate([h, sums.astype(BF16)], axis=0))
        new = h.astype(F32) + norm_columns(mm(wn2[l], half_silu(pre).astype(BF16)))
        new = jnp.where(filled, new, 0.0)
        for copy in copies:
            copy.wait_send()
        for copy in back:
            copy.wait_send()
        if l + 1 < LAYERS:
            h = new.astype(BF16)
        else:
            out[...] = new.T.astype(BF16)


def solution(mesh):
    nx, ny = mesh.shape["gx"], mesh.shape["gy"]

    def shards(
        flow_field,
        enc_first,
        enc_second,
        send_rows,
        part_sizes,
        halo_rows,
        neighbours,
        edge_first,
        edge_second,
        node_first,
        node_second,
    ):
        del part_sizes
        vmem = pl.BlockSpec(memory_space=pltpu.VMEM)
        dma = pltpu.SemaphoreType.DMA
        operands = (
            flow_field,
            jnp.asarray(interp_parts()),
            jnp.transpose(send_rows, (0, 2, 1)),
            neighbours,
            halo_rows,
            enc_first,
            enc_second,
            edge_first,
            edge_second,
            node_first,
            node_second,
        )
        return pl.pallas_call(
            functools.partial(kernel, nx, ny),
            out_shape=jax.ShapeDtypeStruct((NODES, D), BF16),
            in_specs=[pl.BlockSpec(memory_space=pltpu.HBM)] * 11,
            out_specs=vmem,
            scratch_shapes=[
                *[pltpu.VMEM(x.shape, x.dtype) for x in operands],
                pltpu.VMEM((ROWS, EDGES), F8),
                pltpu.VMEM((2 * D, EDGES), F8),
                pltpu.VMEM((D, EDGES), BF16),
                pltpu.VMEM((STEPS, D, CH), F32),
                pltpu.VMEM((2 * D, ROWS), F8),
                pltpu.VMEM((NODES, HALO), BF16),
                pltpu.VMEM((NODES, 2 * D), BF16),
                pltpu.VMEM((LAYERS, D, D), BF16),
                pltpu.VMEM((LAYERS, D, D), BF16),
                pltpu.VMEM((LAYERS, D, D), BF16),
                pltpu.VMEM((LAYERS, D, D), BF16),
                pltpu.VMEM((LAYERS, D, 2 * D), BF16),
                pltpu.VMEM((LAYERS, D, D), BF16),
                pltpu.VMEM((2 * D + 16, 2 * D), BF16),
                pltpu.VMEM((D, D), BF16),
                pltpu.VMEM((D, NODES), F32),
                pltpu.VMEM((D, D), jnp.int32),
                pltpu.VMEM((ny, nx, D), F32),
                pltpu.VMEM((ny, nx, D), F32),
                pltpu.VMEM((nx, ny, D), F32),
                pltpu.VMEM((nx, ny, D), F32),
                pltpu.VMEM((LAYERS, 4, D, D), BF16),
                pltpu.VMEM((LAYERS, 4, D, D), BF16),
                pltpu.VMEM((LAYERS, 4, D, D), BF16),
                pltpu.VMEM((LAYERS, 4, D, D), BF16),
                dma((len(operands),)),
                dma((ny - 1,)),
                dma((ny - 1,)),
                dma((nx - 1,)),
                dma((nx - 1,)),
                dma((LAYERS, 4)),
                dma((LAYERS, 4)),
                dma((LAYERS, 4)),
                dma((LAYERS, 4)),
            ],
            compiler_params=pltpu.CompilerParams(
                collective_id=0, has_side_effects=True, vmem_limit_bytes=60 << 20
            ),
        )(*operands)

    in_specs = (
        P(("gx", "gy"), None, None),
        P(),
        P(),
        P(("gx", "gy"), None, None),
        P(("gx", "gy"), None),
        P(("gx", "gy"), None, None, None),
        P(None, ("gx", "gy")),
        P(),
        P(),
        P(),
        P(),
    )
    out_specs = P(("gx", "gy"), None)
    return jax.shard_map(shards, mesh=mesh, in_specs=in_specs, out_specs=out_specs, check_vma=False)
```

```python
import functools

import jax
import jax.numpy as jnp
import numpy as np
from jax import lax
from jax.experimental import pallas as pl
from jax.experimental.pallas import tpu as pltpu
from jax.sharding import PartitionSpec as P

MESH = pl.DeviceIdType.MESH
F32 = jnp.float32
BF16 = jnp.bfloat16
F8 = jnp.float8_e4m3fn

LAYERS = 2
GLL_POINTS = (
    -1.0,
    -0.8717401485096066,
    -0.5917001814331423,
    -0.2092992179024789,
    0.2092992179024789,
    0.5917001814331423,
    0.8717401485096066,
    1.0,
)
EPS = 1e-05
D = 128
NODES = 1024
HALO = 512
ROWS = NODES + HALO
FAR = NODES + HALO // 2
SLOTS = 8
EDGES = SLOTS * NODES
GROUP = 4
CH = GROUP * NODES
STEPS = SLOTS // GROUP


def interp_table():
    gll_nodes = np.array(GLL_POINTS)
    targets = np.array([-0.75, -0.25, 0.25, 0.75])
    basis_line = np.ones((4, 8))
    for j in range(8):
        for m in range(8):
            if m != j:
                basis_line[:, j] *= (targets - gll_nodes[m]) / (gll_nodes[j] - gll_nodes[m])
    return np.kron(np.kron(basis_line, basis_line), basis_line).astype(np.float32)


def interp_parts():
    table = interp_table()
    high = table.astype(BF16)
    low = (table - high.astype(np.float32)).astype(BF16)
    return np.concatenate([high, low], axis=0)


def mm(a, b):
    return jnp.dot(a, b, preferred_element_type=F32)


def mm_t(a, b):
    return lax.dot_general(a, b, (((1,), (1,)), ((), ())), preferred_element_type=F32)


def two_terms(x, dtype):
    high = x.astype(dtype)
    return high, (x - high.astype(F32)).astype(dtype)


def half_silu(u):
    return u + u * jnp.tanh(u)


def norm_columns(v, scale=1.0):
    spread = jnp.sum(v * v, axis=0, keepdims=True) * (1.0 / D)
    return v * (lax.rsqrt(spread + EPS) * scale)


def centred_t(w):
    w = w.astype(F32)
    return (w - jnp.mean(w, axis=1, keepdims=True)).T.astype(BF16)


def scaled_t(w, scale):
    return (w.astype(F32).T * scale).astype(BF16)


def kernel(
    nx,
    ny,
    flow_hbm,
    interp_hbm,
    send_hbm,
    links_hbm,
    halo_hbm,
    enc_first_hbm,
    enc_second_hbm,
    edge_first_hbm,
    edge_second_hbm,
    node_first_hbm,
    node_second_hbm,
    out,
    flow,
    interp,
    send_rows,
    links,
    halo,
    enc_first,
    enc_second,
    edge_first,
    edge_second,
    node_first,
    node_second,
    oht,
    e8,
    e16,
    part,
    t8,
    ohh,
    xs,
    wsrc,
    wown,
    wdst,
    we2,
    wn1,
    wn2,
    wenc1,
    wenc2,
    src,
    ordered,
    sbuf,
    r1,
    mid,
    r2,
    hsend,
    hrecv,
    bsend,
    brecv,
    loads,
    s1,
    q1,
    s2,
    q2,
    fs,
    fq,
    bs,
    bq,
):
    gx, gy = lax.axis_index("gx"), lax.axis_index("gy")

    def at_x(step):
        return (lax.rem(gx + (step + nx), nx), gy)

    def at_y(step):
        return (gx, lax.rem(gy + (step + ny), ny))

    pairs = (
        (flow_hbm, flow),
        (interp_hbm, interp),
        (send_hbm, send_rows),
        (links_hbm, links),
        (halo_hbm, halo),
        (enc_first_hbm, enc_first),
        (enc_second_hbm, enc_second),
        (edge_first_hbm, edge_first),
        (edge_second_hbm, edge_second),
        (node_first_hbm, node_first),
        (node_second_hbm, node_second),
    )
    loading = [
        pltpu.make_async_copy(there, here, loads.at[i]) for i, (there, here) in enumerate(pairs)
    ]
    for copy in loading:
        copy.start()
    barrier = pltpu.get_barrier_semaphore()
    for step in range(1, ny):
        pl.semaphore_signal(barrier, inc=1, device_id=at_y(step), device_id_type=MESH)
    for step in range(1, nx):
        pl.semaphore_signal(barrier, inc=1, device_id=at_x(step), device_id_type=MESH)
    for copy in loading[:3]:
        copy.wait()

    tiles = []
    for e in range(8):
        f = flow[e]
        f = jnp.concatenate([f, f], axis=0)
        tiles.append(jnp.concatenate([f, f, f, f], axis=0))
    flow_high, flow_low = two_terms(jnp.concatenate(tiles, axis=0), BF16)
    main = mm_t(interp[...], flow_high)
    sampled = main[:64] + main[64:] + mm_t(interp[0:64, :], flow_low)
    columns = jnp.concatenate([sampled[:, 32 * e : 32 * e + 32] for e in range(8)], axis=0)
    col_high, col_low = two_terms(columns, BF16)
    table = jnp.concatenate(
        [
            col_high,
            jnp.ones((512, 8), BF16),
            jnp.zeros((512, 88), BF16),
            col_low,
            jnp.zeros((512, 96), BF16),
        ],
        axis=1,
    )
    lane = lax.broadcasted_iota(jnp.int32, (D, D), 1)
    picked = jnp.zeros((D, D), F32)
    ordered[...] = jnp.concatenate([send_rows[0]] * 16, axis=0).T
    slots = jnp.concatenate(
        [ordered[pl.ds(y, nx, stride=ny), :] for y in range(ny)], axis=0
    )
    node_ids = lax.broadcasted_iota(jnp.int32, (D, 512), 1)
    for k in range(SLOTS):
        choose = (slots[:, k : k + 1] == node_ids).astype(F32).astype(BF16)
        both = mm(choose, table)
        mine = ((lane < 32) & (lane // 4 == k)) | (lane == 32 + k)
        picked = picked + jnp.where(mine, both[:, :D] + both[:, D:], 0.0)
    for y in range(ny):
        sbuf[y] = picked[y * nx : y * nx + nx, :]

    pl.semaphore_wait(barrier, nx + ny - 2)

    first = []
    for step in range(1, ny):
        target = at_y(step)
        copy = pltpu.make_async_remote_copy(
            src_ref=sbuf.at[target[1]],
            dst_ref=r1.at[gy],
            send_sem=s1.at[step - 1],
            recv_sem=q1.at[step - 1],
            device_id=target,
            device_id_type=MESH,
        )
        copy.start()
        first.append(copy)
    r1[gy] = sbuf[gy]
    for copy in loading[3:]:
        copy.wait()

    sub8 = lax.broadcasted_iota(jnp.int32, (D, NODES), 0).astype(jnp.int8)

    def make_oht(k, carry):
        ids = links[pl.ds(k, 1), :]
        where = pl.ds(pl.multiple_of(k * NODES, NODES), NODES)
        for a in range(ROWS // D):
            key = ids - D * a
            key = jnp.where((key >= 0) & (key < D), key, -1).astype(jnp.int8)
            oht[pl.ds(a * D, D), where] = jnp.where(
                key == sub8, jnp.full((), 0.125, F8), jnp.zeros((), F8)
            )
        return carry

    lax.fori_loop(0, SLOTS // 2, make_oht, 0)

    for copy in first:
        copy.wait_recv()
    for x in range(nx):
        mid[x] = r1[:, x, :]
    second = []
    for step in range(1, nx):
        target = at_x(step)
        copy = pltpu.make_async_remote_copy(
            src_ref=mid.at[target[0]],
            dst_ref=r2.at[gx],
            send_sem=s2.at[step - 1],
            recv_sem=q2.at[step - 1],
            device_id=target,
            device_id_type=MESH,
        )
        copy.start()
        second.append(copy)
    r2[gx] = mid[gx]

    lax.fori_loop(SLOTS // 2, SLOTS, make_oht, 0)

    spread_first = jnp.concatenate([enc_first[...], enc_first[...]], axis=0)
    spread_first = jnp.concatenate([spread_first] * 16, axis=0).T
    enc_high, enc_low = two_terms(jnp.where(lane < 32, spread_first * 0.5, 0.0), BF16)
    wenc1[0:D, 0:D] = enc_high
    wenc1[0:D, D : 2 * D] = enc_high
    wenc1[D : 2 * D, 0:D] = enc_low
    wenc1[D : 2 * D, D : 2 * D] = jnp.zeros((D, D), BF16)
    mark = lax.broadcasted_iota(jnp.int32, (16, 2 * D), 1)
    wenc1[2 * D : 2 * D + 16, :] = ((mark >= 32) & (mark < 40)).astype(F32).astype(BF16)
    wenc2[...] = centred_t(enc_second[...])
    for l in range(LAYERS):
        wown[l] = scaled_t(edge_first[l, 0:D, :], 0.03125)
        wsrc[l] = scaled_t(edge_first[l, D : 2 * D, :], 0.5)
        wdst[l] = scaled_t(edge_first[l, 2 * D : 3 * D, :], 4.0)
        we2[l] = centred_t(edge_second[l])
        wn1[l, :, 0:D] = scaled_t(node_first[l, 0:D, :], 0.5)
        wn1[l, :, D : 2 * D] = scaled_t(node_first[l, D : 2 * D, :], 0.5)
        wn2[l] = centred_t(node_second[l])

    node_rows = lax.broadcasted_iota(jnp.int32, (NODES, D), 0)
    for j, (p, q) in enumerate((((1, 0), (1, 1)), ((0, 0), (0, 1)), ((0, 1), (1, 1)), ((0, 0), (1, 0)))):
        ids = jnp.concatenate([halo[0, p[0], p[1] : p[1] + 1, :], halo[0, q[0], q[1] : q[1] + 1, :]], axis=1)
        ohh[:, D * j : D * j + D] = (ids == node_rows).astype(F32).astype(BF16)

    for copy in first:
        copy.wait_send()
    for copy in second:
        copy.wait_recv()

    sub = lax.broadcasted_iota(jnp.int32, (8, D), 0)
    lane8 = lax.broadcasted_iota(jnp.int32, (8, D), 1)
    keep = ((lane8 < 32) & (lane8 // 4 == sub)) | (lane8 == 32 + sub)
    for x in range(nx):
        for y in range(0, ny, 2):
            rows = jnp.concatenate(
                [
                    jnp.where(keep, jnp.broadcast_to(r2[x, y : y + 1, :], (8, D)), 0.0),
                    jnp.where(keep, jnp.broadcast_to(r2[x, y + 1 : y + 2, :], (8, D)), 0.0),
                ],
                axis=0,
            )
            high, low = two_terms(rows, BF16)
            base = (x * ny + y) * 8
            xs[base : base + 16, 0:D] = high
            xs[base : base + 16, D : 2 * D] = low
    pre = mm_t(wenc1[...], xs[...])
    filled = pre[2 * D : 2 * D + 1, :] > 0.5
    hidden = half_silu(pre[:D] + pre[D : 2 * D]).astype(BF16)
    h = norm_columns(mm(wenc2[...], hidden))
    h = jnp.where(filled, h, 0.0).astype(BF16)
    for copy in second:
        copy.wait_send()

    forward = (at_x(1), at_x(-1), at_y(1), at_y(-1))
    backward = (at_x(-1), at_x(1), at_y(-1), at_y(1))

    for l in range(LAYERS):
        proj = mm(wdst[l], h)
        rounded = proj.astype(BF16)
        copies = []
        for j in range(4):
            if j % 2 == 0:
                border = mm(rounded, ohh[:, D * j : D * j + 2 * D]).astype(BF16)
            hsend[l, j] = border[:, D * (j % 2) : D * (j % 2) + D]
            copy = pltpu.make_async_remote_copy(
                src_ref=hsend.at[l, j],
                dst_ref=hrecv.at[l, j],
                send_sem=fs.at[l, j],
                recv_sem=fq.at[l, j],
                device_id=forward[j],
                device_id_type=MESH,
            )
            copy.start()
            copies.append(copy)
        high, low = two_terms(proj, F8)
        t8[0:D, 0:NODES] = high
        t8[D : 2 * D, 0:NODES] = low
        src[...] = mm(wsrc[l], h)

        def local_step(c, carry):
            where = pl.ds(pl.multiple_of(c * CH, CH), CH)
            got = mm(t8[:, 0:NODES], oht[0:NODES, where])
            u = got[:D] + got[D:] + jnp.concatenate([src[...]] * GROUP, axis=1)
            if l > 0:
                u = u + mm(wown[l], e16[:, where])
            part[c] = u
            return carry

        lax.fori_loop(0, STEPS, local_step, 0, unroll=2)

        def take(j):
            copies[j].wait_recv()
            high, low = two_terms(hrecv[l, j].astype(F32), F8)
            t8[0:D, NODES + D * j : NODES + D * j + D] = high
            t8[D : 2 * D, NODES + D * j : NODES + D * j + D] = low

        take(2)
        take(3)

        def near_step(c, carry):
            where = pl.ds(pl.multiple_of(c * CH, CH), CH)
            got = mm(t8[:, FAR:ROWS], oht[FAR:ROWS, where])
            part[c] = part[c] + got[:D] + got[D:]
            return carry

        lax.fori_loop(0, STEPS, near_step, 0, unroll=2)
        take(0)
        take(1)

        def edge_step(c, carry):
            where = pl.ds(pl.multiple_of(c * CH, CH), CH)
            got = mm(t8[:, NODES:FAR], oht[NODES:FAR, where])
            u = (part[c] + got[:D] + got[D:]).astype(BF16)
            new = norm_columns(mm(we2[l], half_silu(u)), 16.0).astype(BF16)
            if l > 0:
                new = new + e16[:, where]
            if l + 1 < LAYERS:
                e16[:, where] = new
            high = new.astype(F8)
            e8[0:D, where] = high
            e8[D : 2 * D, where] = (new - high.astype(BF16)).astype(F8)
            return carry

        lax.fori_loop(0, STEPS, edge_step, 0, unroll=2)

        sums = mm_t(e8[...], oht[NODES:ROWS, :])
        sums = ((sums[:D] + sums[D:]) * 0.5).astype(BF16)
        back = []
        for j in range(4):
            bsend[l, j] = sums[:, D * j : D * j + D]
            copy = pltpu.make_async_remote_copy(
                src_ref=bsend.at[l, j],
                dst_ref=brecv.at[l, j],
                send_sem=bs.at[l, j],
                recv_sem=bq.at[l, j],
                device_id=backward[j],
                device_id_type=MESH,
            )
            copy.start()
            back.append(copy)
        sums = mm_t(e8[...], oht[0:NODES, :])
        sums = (sums[:D] + sums[D:]) * 0.5
        for j in (2, 0):
            back[j].wait_recv()
            back[j + 1].wait_recv()
            returned = jnp.concatenate([brecv[l, j], brecv[l, j + 1]], axis=1)
            sums = sums + mm_t(returned, ohh[:, D * j : D * j + 2 * D])
        pre = mm(wn1[l], jnp.concatenate([h, sums.astype(BF16)], axis=0))
        new = h.astype(F32) + norm_columns(mm(wn2[l], half_silu(pre).astype(BF16)))
        new = jnp.where(filled, new, 0.0)
        for copy in copies:
            copy.wait_send()
        for copy in back:
            copy.wait_send()
        if l + 1 < LAYERS:
            h = new.astype(BF16)
        else:
            out[...] = new.T.astype(BF16)


def solution(mesh):
    nx, ny = mesh.shape["gx"], mesh.shape["gy"]

    def shards(
        flow_field,
        enc_first,
        enc_second,
        send_rows,
        part_sizes,
        halo_rows,
        neighbours,
        edge_first,
        edge_second,
        node_first,
        node_second,
    ):
        del part_sizes
        vmem = pl.BlockSpec(memory_space=pltpu.VMEM)
        dma = pltpu.SemaphoreType.DMA
        operands = (
            flow_field,
            jnp.asarray(interp_parts()),
            jnp.transpose(send_rows, (0, 2, 1)),
            neighbours,
            halo_rows,
            enc_first,
            enc_second,
            edge_first,
            edge_second,
            node_first,
            node_second,
        )
        return pl.pallas_call(
            functools.partial(kernel, nx, ny),
            out_shape=jax.ShapeDtypeStruct((NODES, D), BF16),
            in_specs=[pl.BlockSpec(memory_space=pltpu.HBM)] * 11,
            out_specs=vmem,
            scratch_shapes=[
                *[pltpu.VMEM(x.shape, x.dtype) for x in operands],
                pltpu.VMEM((ROWS, EDGES), F8),
                pltpu.VMEM((2 * D, EDGES), F8),
                pltpu.VMEM((D, EDGES), BF16),
                pltpu.VMEM((STEPS, D, CH), F32),
                pltpu.VMEM((2 * D, ROWS), F8),
                pltpu.VMEM((NODES, HALO), BF16),
                pltpu.VMEM((NODES, 2 * D), BF16),
                pltpu.VMEM((LAYERS, D, D), BF16),
                pltpu.VMEM((LAYERS, D, D), BF16),
                pltpu.VMEM((LAYERS, D, D), BF16),
                pltpu.VMEM((LAYERS, D, D), BF16),
                pltpu.VMEM((LAYERS, D, 2 * D), BF16),
                pltpu.VMEM((LAYERS, D, D), BF16),
                pltpu.VMEM((2 * D + 16, 2 * D), BF16),
                pltpu.VMEM((D, D), BF16),
                pltpu.VMEM((D, NODES), F32),
                pltpu.VMEM((D, D), jnp.int32),
                pltpu.VMEM((ny, nx, D), F32),
                pltpu.VMEM((ny, nx, D), F32),
                pltpu.VMEM((nx, ny, D), F32),
                pltpu.VMEM((nx, ny, D), F32),
                pltpu.VMEM((LAYERS, 4, D, D), BF16),
                pltpu.VMEM((LAYERS, 4, D, D), BF16),
                pltpu.VMEM((LAYERS, 4, D, D), BF16),
                pltpu.VMEM((LAYERS, 4, D, D), BF16),
                dma((len(operands),)),
                dma((ny - 1,)),
                dma((ny - 1,)),
                dma((nx - 1,)),
                dma((nx - 1,)),
                dma((LAYERS, 4)),
                dma((LAYERS, 4)),
                dma((LAYERS, 4)),
                dma((LAYERS, 4)),
            ],
            compiler_params=pltpu.CompilerParams(
                collective_id=0, has_side_effects=True, vmem_limit_bytes=60 << 20
            ),
        )(*operands)

    in_specs = (
        P(("gx", "gy"), None, None),
        P(),
        P(),
        P(("gx", "gy"), None, None),
        P(("gx", "gy"), None),
        P(("gx", "gy"), None, None, None),
        P(None, ("gx", "gy")),
        P(),
        P(),
        P(),
        P(),
    )
    out_specs = P(("gx", "gy"), None)
    return jax.shard_map(shards, mesh=mesh, in_specs=in_specs, out_specs=out_specs, check_vma=False)
```

```python
import functools

import jax
import jax.numpy as jnp
import numpy as np
from jax import lax
from jax.experimental import pallas as pl
from jax.experimental.pallas import tpu as pltpu
from jax.sharding import PartitionSpec as P

MESH = pl.DeviceIdType.MESH
F32 = jnp.float32
BF16 = jnp.bfloat16
F8 = jnp.float8_e4m3fn

LAYERS = 2
GLL_POINTS = (
    -1.0,
    -0.8717401485096066,
    -0.5917001814331423,
    -0.2092992179024789,
    0.2092992179024789,
    0.5917001814331423,
    0.8717401485096066,
    1.0,
)
EPS = 1e-05
D = 128
NODES = 1024
HALO = 512
ROWS = NODES + HALO
FAR = NODES + HALO // 2
SLOTS = 8
EDGES = SLOTS * NODES
GROUP = 4
CH = GROUP * NODES
STEPS = SLOTS // GROUP


def interp_table():
    gll_nodes = np.array(GLL_POINTS)
    targets = np.array([-0.75, -0.25, 0.25, 0.75])
    basis_line = np.ones((4, 8))
    for j in range(8):
        for m in range(8):
            if m != j:
                basis_line[:, j] *= (targets - gll_nodes[m]) / (gll_nodes[j] - gll_nodes[m])
    return np.kron(np.kron(basis_line, basis_line), basis_line).astype(np.float32)


def interp_parts():
    table = interp_table()
    high = table.astype(BF16)
    low = (table - high.astype(np.float32)).astype(BF16)
    return np.concatenate([high, low], axis=0)


def hops(step, around):
    return min(step, around - step)


def mm(a, b):
    return jnp.dot(a, b, preferred_element_type=F32)


def mm_t(a, b):
    return lax.dot_general(a, b, (((1,), (1,)), ((), ())), preferred_element_type=F32)


def two_terms(x, dtype):
    high = x.astype(dtype)
    return high, (x - high.astype(F32)).astype(dtype)


def half_silu(u):
    return u + u * jnp.tanh(u)


def norm_columns(v, scale=1.0):
    spread = jnp.sum(v * v, axis=0, keepdims=True) * (1.0 / D)
    return v * (lax.rsqrt(spread + EPS) * scale)


def centred_t(w):
    w = w.astype(F32)
    return (w - jnp.mean(w, axis=1, keepdims=True)).T.astype(BF16)


def scaled_t(w, scale):
    return (w.astype(F32).T * scale).astype(BF16)


def kernel(
    nx,
    ny,
    flow_hbm,
    interp_hbm,
    send_hbm,
    links_hbm,
    halo_hbm,
    enc_first_hbm,
    enc_second_hbm,
    edge_first_hbm,
    edge_second_hbm,
    node_first_hbm,
    node_second_hbm,
    out,
    flow,
    interp,
    send_rows,
    links,
    halo,
    enc_first,
    enc_second,
    edge_first,
    edge_second,
    node_first,
    node_second,
    oht,
    e8,
    e16,
    part,
    t8,
    ohh,
    xs,
    wsrc,
    wown,
    wdst,
    we2,
    wn1,
    wn2,
    wenc1,
    wenc2,
    src,
    ordered,
    sbuf,
    r1,
    mid,
    r2,
    hsend,
    hrecv,
    bsend,
    brecv,
    loads,
    s1,
    q1,
    s2,
    q2,
    fs,
    fq,
    bs,
    bq,
):
    gx, gy = lax.axis_index("gx"), lax.axis_index("gy")

    def at_x(step):
        return (lax.rem(gx + (step + nx), nx), gy)

    def at_y(step):
        return (gx, lax.rem(gy + (step + ny), ny))

    barrier = pltpu.get_barrier_semaphore()
    x_steps = sorted(range(1, nx), key=lambda s: -hops(s % 4, 4) - hops(s // 4, nx // 4))
    y_steps = sorted(range(1, ny), key=lambda s: -hops(s, ny))
    for step in x_steps:
        pl.semaphore_signal(barrier, inc=1, device_id=at_x(step), device_id_type=MESH)
    for step in y_steps:
        pl.semaphore_signal(barrier, inc=1, device_id=at_y(step), device_id_type=MESH)

    pairs = (
        (flow_hbm, flow),
        (interp_hbm, interp),
        (send_hbm, send_rows),
        (links_hbm, links),
        (halo_hbm, halo),
        (enc_first_hbm, enc_first),
        (enc_second_hbm, enc_second),
        (edge_first_hbm, edge_first),
        (edge_second_hbm, edge_second),
        (node_first_hbm, node_first),
        (node_second_hbm, node_second),
    )
    loading = [
        pltpu.make_async_copy(there, here, loads.at[i]) for i, (there, here) in enumerate(pairs)
    ]
    for copy in loading:
        copy.start()
    for copy in loading[:3]:
        copy.wait()

    tiles = []
    for e in range(8):
        f = flow[e]
        f = jnp.concatenate([f, f], axis=0)
        tiles.append(jnp.concatenate([f, f, f, f], axis=0))
    flow_high, flow_low = two_terms(jnp.concatenate(tiles, axis=0), BF16)
    main = mm_t(interp[...], flow_high)
    sampled = main[:64] + main[64:] + mm_t(interp[0:64, :], flow_low)
    columns = jnp.concatenate([sampled[:, 32 * e : 32 * e + 32] for e in range(8)], axis=0)
    col_high, col_low = two_terms(columns, BF16)
    table = jnp.concatenate(
        [
            col_high,
            jnp.ones((512, 8), BF16),
            jnp.zeros((512, 88), BF16),
            col_low,
            jnp.zeros((512, 96), BF16),
        ],
        axis=1,
    )
    lane = lax.broadcasted_iota(jnp.int32, (D, D), 1)
    picked = jnp.zeros((D, D), F32)
    ordered[...] = jnp.concatenate([send_rows[0]] * 16, axis=0).T
    slots = jnp.concatenate(
        [ordered[pl.ds(y, nx, stride=ny), :] for y in range(ny)], axis=0
    )
    node_ids = lax.broadcasted_iota(jnp.int32, (D, 512), 1)
    for k in range(SLOTS):
        choose = (slots[:, k : k + 1] == node_ids).astype(F32).astype(BF16)
        both = mm(choose, table)
        mine = ((lane < 32) & (lane // 4 == k)) | (lane == 32 + k)
        picked = picked + jnp.where(mine, both[:, :D] + both[:, D:], 0.0)
    for y in range(ny):
        sbuf[y] = picked[y * nx : y * nx + nx, :]

    pl.semaphore_wait(barrier, nx + ny - 2)

    first = []
    for step in y_steps:
        target = at_y(step)
        copy = pltpu.make_async_remote_copy(
            src_ref=sbuf.at[target[1]],
            dst_ref=r1.at[gy],
            send_sem=s1.at[step - 1],
            recv_sem=q1.at[step - 1],
            device_id=target,
            device_id_type=MESH,
        )
        copy.start()
        first.append(copy)
    r1[gy] = sbuf[gy]
    for copy in loading[3:]:
        copy.wait()

    sub8 = lax.broadcasted_iota(jnp.int32, (D, NODES), 0).astype(jnp.int8)

    def make_oht(k, carry):
        ids = links[pl.ds(k, 1), :]
        where = pl.ds(pl.multiple_of(k * NODES, NODES), NODES)
        for a in range(ROWS // D):
            key = ids - D * a
            key = jnp.where((key >= 0) & (key < D), key, -1).astype(jnp.int8)
            oht[pl.ds(a * D, D), where] = jnp.where(
                key == sub8, jnp.full((), 0.125, F8), jnp.zeros((), F8)
            )
        return carry

    lax.fori_loop(0, SLOTS // 2, make_oht, 0)

    for copy in first:
        copy.wait_recv()
    for x in range(nx):
        mid[x] = r1[:, x, :]
    second = []
    for step in x_steps:
        target = at_x(step)
        copy = pltpu.make_async_remote_copy(
            src_ref=mid.at[target[0]],
            dst_ref=r2.at[gx],
            send_sem=s2.at[step - 1],
            recv_sem=q2.at[step - 1],
            device_id=target,
            device_id_type=MESH,
        )
        copy.start()
        second.append(copy)
    r2[gx] = mid[gx]

    lax.fori_loop(SLOTS // 2, SLOTS, make_oht, 0)

    spread_first = jnp.concatenate([enc_first[...], enc_first[...]], axis=0)
    spread_first = jnp.concatenate([spread_first] * 16, axis=0).T
    enc_high, enc_low = two_terms(jnp.where(lane < 32, spread_first * 0.5, 0.0), BF16)
    wenc1[0:D, 0:D] = enc_high
    wenc1[0:D, D : 2 * D] = enc_high
    wenc1[D : 2 * D, 0:D] = enc_low
    wenc1[D : 2 * D, D : 2 * D] = jnp.zeros((D, D), BF16)
    mark = lax.broadcasted_iota(jnp.int32, (16, 2 * D), 1)
    wenc1[2 * D : 2 * D + 16, :] = ((mark >= 32) & (mark < 40)).astype(F32).astype(BF16)
    wenc2[...] = centred_t(enc_second[...])
    for l in range(LAYERS):
        wown[l] = scaled_t(edge_first[l, 0:D, :], 0.03125)
        wsrc[l] = scaled_t(edge_first[l, D : 2 * D, :], 0.5)
        wdst[l] = scaled_t(edge_first[l, 2 * D : 3 * D, :], 4.0)
        we2[l] = centred_t(edge_second[l])
        wn1[l, :, 0:D] = scaled_t(node_first[l, 0:D, :], 0.5)
        wn1[l, :, D : 2 * D] = scaled_t(node_first[l, D : 2 * D, :], 0.5)
        wn2[l] = centred_t(node_second[l])

    node_rows = lax.broadcasted_iota(jnp.int32, (NODES, D), 0)
    for j, (p, q) in enumerate((((1, 0), (1, 1)), ((0, 0), (0, 1)), ((0, 1), (1, 1)), ((0, 0), (1, 0)))):
        ids = jnp.concatenate([halo[0, p[0], p[1] : p[1] + 1, :], halo[0, q[0], q[1] : q[1] + 1, :]], axis=1)
        ohh[:, D * j : D * j + D] = (ids == node_rows).astype(F32).astype(BF16)

    for copy in first:
        copy.wait_send()
    for copy in second:
        copy.wait_recv()

    sub = lax.broadcasted_iota(jnp.int32, (8, D), 0)
    lane8 = lax.broadcasted_iota(jnp.int32, (8, D), 1)
    keep = ((lane8 < 32) & (lane8 // 4 == sub)) | (lane8 == 32 + sub)
    for x in range(nx):
        for y in range(0, ny, 2):
            rows = jnp.concatenate(
                [
                    jnp.where(keep, jnp.broadcast_to(r2[x, y : y + 1, :], (8, D)), 0.0),
                    jnp.where(keep, jnp.broadcast_to(r2[x, y + 1 : y + 2, :], (8, D)), 0.0),
                ],
                axis=0,
            )
            high, low = two_terms(rows, BF16)
            base = (x * ny + y) * 8
            xs[base : base + 16, 0:D] = high
            xs[base : base + 16, D : 2 * D] = low
    pre = mm_t(wenc1[...], xs[...])
    filled = pre[2 * D : 2 * D + 1, :] > 0.5
    hidden = half_silu(pre[:D] + pre[D : 2 * D]).astype(BF16)
    h = norm_columns(mm(wenc2[...], hidden))
    h = jnp.where(filled, h, 0.0).astype(BF16)
    for copy in second:
        copy.wait_send()

    forward = (at_x(1), at_x(-1), at_y(1), at_y(-1))
    backward = (at_x(-1), at_x(1), at_y(-1), at_y(1))

    for l in range(LAYERS):
        proj = mm(wdst[l], h)
        rounded = proj.astype(BF16)
        copies = []
        for j in range(4):
            if j % 2 == 0:
                border = mm(rounded, ohh[:, D * j : D * j + 2 * D]).astype(BF16)
            hsend[l, j] = border[:, D * (j % 2) : D * (j % 2) + D]
            copy = pltpu.make_async_remote_copy(
                src_ref=hsend.at[l, j],
                dst_ref=hrecv.at[l, j],
                send_sem=fs.at[l, j],
                recv_sem=fq.at[l, j],
                device_id=forward[j],
                device_id_type=MESH,
            )
            copy.start()
            copies.append(copy)
        high, low = two_terms(proj, F8)
        t8[0:D, 0:NODES] = high
        t8[D : 2 * D, 0:NODES] = low
        src[...] = mm(wsrc[l], h)

        def local_step(c, carry):
            where = pl.ds(pl.multiple_of(c * CH, CH), CH)
            got = mm(t8[:, 0:NODES], oht[0:NODES, where])
            u = got[:D] + got[D:] + jnp.concatenate([src[...]] * GROUP, axis=1)
            if l > 0:
                u = u + mm(wown[l], e16[:, where])
            part[c] = u
            return carry

        lax.fori_loop(0, STEPS, local_step, 0, unroll=2)

        def take(j):
            copies[j].wait_recv()
            high, low = two_terms(hrecv[l, j].astype(F32), F8)
            t8[0:D, NODES + D * j : NODES + D * j + D] = high
            t8[D : 2 * D, NODES + D * j : NODES + D * j + D] = low

        take(2)
        take(3)

        def near_step(c, carry):
            where = pl.ds(pl.multiple_of(c * CH, CH), CH)
            got = mm(t8[:, FAR:ROWS], oht[FAR:ROWS, where])
            part[c] = part[c] + got[:D] + got[D:]
            return carry

        lax.fori_loop(0, STEPS, near_step, 0, unroll=2)
        take(0)
        take(1)

        def edge_step(c, carry):
            where = pl.ds(pl.multiple_of(c * CH, CH), CH)
            got = mm(t8[:, NODES:FAR], oht[NODES:FAR, where])
            u = (part[c] + got[:D] + got[D:]).astype(BF16)
            new = norm_columns(mm(we2[l], half_silu(u)), 16.0).astype(BF16)
            if l > 0:
                new = new + e16[:, where]
            if l + 1 < LAYERS:
                e16[:, where] = new
            high = new.astype(F8)
            e8[0:D, where] = high
            e8[D : 2 * D, where] = (new - high.astype(BF16)).astype(F8)
            return carry

        lax.fori_loop(0, STEPS, edge_step, 0, unroll=2)

        sums = mm_t(e8[...], oht[NODES:ROWS, :])
        sums = ((sums[:D] + sums[D:]) * 0.5).astype(BF16)
        back = []
        for j in range(4):
            bsend[l, j] = sums[:, D * j : D * j + D]
            copy = pltpu.make_async_remote_copy(
                src_ref=bsend.at[l, j],
                dst_ref=brecv.at[l, j],
                send_sem=bs.at[l, j],
                recv_sem=bq.at[l, j],
                device_id=backward[j],
                device_id_type=MESH,
            )
            copy.start()
            back.append(copy)
        sums = mm_t(e8[...], oht[0:NODES, :])
        sums = (sums[:D] + sums[D:]) * 0.5
        for j in (2, 0):
            back[j].wait_recv()
            back[j + 1].wait_recv()
            returned = jnp.concatenate([brecv[l, j], brecv[l, j + 1]], axis=1)
            sums = sums + mm_t(returned, ohh[:, D * j : D * j + 2 * D])
        pre = mm(wn1[l], jnp.concatenate([h, sums.astype(BF16)], axis=0))
        new = h.astype(F32) + norm_columns(mm(wn2[l], half_silu(pre).astype(BF16)))
        new = jnp.where(filled, new, 0.0)
        for copy in copies:
            copy.wait_send()
        for copy in back:
            copy.wait_send()
        if l + 1 < LAYERS:
            h = new.astype(BF16)
        else:
            out[...] = new.T.astype(BF16)


def solution(mesh):
    nx, ny = mesh.shape["gx"], mesh.shape["gy"]

    def shards(
        flow_field,
        enc_first,
        enc_second,
        send_rows,
        part_sizes,
        halo_rows,
        neighbours,
        edge_first,
        edge_second,
        node_first,
        node_second,
    ):
        del part_sizes
        vmem = pl.BlockSpec(memory_space=pltpu.VMEM)
        dma = pltpu.SemaphoreType.DMA
        operands = (
            flow_field,
            jnp.asarray(interp_parts()),
            jnp.transpose(send_rows, (0, 2, 1)),
            neighbours,
            halo_rows,
            enc_first,
            enc_second,
            edge_first,
            edge_second,
            node_first,
            node_second,
        )
        return pl.pallas_call(
            functools.partial(kernel, nx, ny),
            out_shape=jax.ShapeDtypeStruct((NODES, D), BF16),
            in_specs=[pl.BlockSpec(memory_space=pltpu.HBM)] * 11,
            out_specs=vmem,
            scratch_shapes=[
                *[pltpu.VMEM(x.shape, x.dtype) for x in operands],
                pltpu.VMEM((ROWS, EDGES), F8),
                pltpu.VMEM((2 * D, EDGES), F8),
                pltpu.VMEM((D, EDGES), BF16),
                pltpu.VMEM((STEPS, D, CH), F32),
                pltpu.VMEM((2 * D, ROWS), F8),
                pltpu.VMEM((NODES, HALO), BF16),
                pltpu.VMEM((NODES, 2 * D), BF16),
                pltpu.VMEM((LAYERS, D, D), BF16),
                pltpu.VMEM((LAYERS, D, D), BF16),
                pltpu.VMEM((LAYERS, D, D), BF16),
                pltpu.VMEM((LAYERS, D, D), BF16),
                pltpu.VMEM((LAYERS, D, 2 * D), BF16),
                pltpu.VMEM((LAYERS, D, D), BF16),
                pltpu.VMEM((2 * D + 16, 2 * D), BF16),
                pltpu.VMEM((D, D), BF16),
                pltpu.VMEM((D, NODES), F32),
                pltpu.VMEM((D, D), jnp.int32),
                pltpu.VMEM((ny, nx, D), F32),
                pltpu.VMEM((ny, nx, D), F32),
                pltpu.VMEM((nx, ny, D), F32),
                pltpu.VMEM((nx, ny, D), F32),
                pltpu.VMEM((LAYERS, 4, D, D), BF16),
                pltpu.VMEM((LAYERS, 4, D, D), BF16),
                pltpu.VMEM((LAYERS, 4, D, D), BF16),
                pltpu.VMEM((LAYERS, 4, D, D), BF16),
                dma((len(operands),)),
                dma((ny - 1,)),
                dma((ny - 1,)),
                dma((nx - 1,)),
                dma((nx - 1,)),
                dma((LAYERS, 4)),
                dma((LAYERS, 4)),
                dma((LAYERS, 4)),
                dma((LAYERS, 4)),
            ],
            compiler_params=pltpu.CompilerParams(
                collective_id=0, has_side_effects=True, vmem_limit_bytes=60 << 20
            ),
        )(*operands)

    in_specs = (
        P(("gx", "gy"), None, None),
        P(),
        P(),
        P(("gx", "gy"), None, None),
        P(("gx", "gy"), None),
        P(("gx", "gy"), None, None, None),
        P(None, ("gx", "gy")),
        P(),
        P(),
        P(),
        P(),
    )
    out_specs = P(("gx", "gy"), None)
    return jax.shard_map(shards, mesh=mesh, in_specs=in_specs, out_specs=out_specs, check_vma=False)
```

```python
import functools

import jax
import jax.numpy as jnp
import numpy as np
from jax import lax
from jax.experimental import pallas as pl
from jax.experimental.pallas import tpu as pltpu
from jax.sharding import PartitionSpec as P

MESH = pl.DeviceIdType.MESH
F32 = jnp.float32
BF16 = jnp.bfloat16
F8 = jnp.float8_e4m3fn

LAYERS = 2
GLL_POINTS = (
    -1.0,
    -0.8717401485096066,
    -0.5917001814331423,
    -0.2092992179024789,
    0.2092992179024789,
    0.5917001814331423,
    0.8717401485096066,
    1.0,
)
EPS = 1e-05
D = 128
NODES = 1024
HALO = 512
ROWS = NODES + HALO
FAR = NODES + HALO // 2
SLOTS = 8
EDGES = SLOTS * NODES
GROUP = 4
CH = GROUP * NODES
STEPS = SLOTS // GROUP


def interp_table():
    gll_nodes = np.array(GLL_POINTS)
    targets = np.array([-0.75, -0.25, 0.25, 0.75])
    basis_line = np.ones((4, 8))
    for j in range(8):
        for m in range(8):
            if m != j:
                basis_line[:, j] *= (targets - gll_nodes[m]) / (gll_nodes[j] - gll_nodes[m])
    return np.kron(np.kron(basis_line, basis_line), basis_line).astype(np.float32)


def interp_parts():
    table = interp_table()
    high = table.astype(BF16)
    low = (table - high.astype(np.float32)).astype(BF16)
    return np.concatenate([high, low], axis=0)


def hops(step, around):
    return min(step, around - step)


def mm(a, b):
    return jnp.dot(a, b, preferred_element_type=F32)


def mm_t(a, b):
    return lax.dot_general(a, b, (((1,), (1,)), ((), ())), preferred_element_type=F32)


def two_terms(x, dtype):
    high = x.astype(dtype)
    return high, (x - high.astype(F32)).astype(dtype)


def half_silu(u):
    return u + u * jnp.tanh(u)


def norm_columns(v, scale=1.0):
    spread = jnp.sum(v * v, axis=0, keepdims=True) * (1.0 / D)
    return v * (lax.rsqrt(spread + EPS) * scale)


def centred_t(w):
    w = w.astype(F32)
    return (w - jnp.mean(w, axis=1, keepdims=True)).T.astype(BF16)


def scaled_t(w, scale):
    return (w.astype(F32).T * scale).astype(BF16)


def kernel(
    nx,
    ny,
    flow_hbm,
    interp_hbm,
    send_hbm,
    links_hbm,
    halo_hbm,
    enc_first_hbm,
    enc_second_hbm,
    edge_first_hbm,
    edge_second_hbm,
    node_first_hbm,
    node_second_hbm,
    out,
    flow,
    interp,
    send_rows,
    links,
    halo,
    enc_first,
    enc_second,
    edge_first,
    edge_second,
    node_first,
    node_second,
    oht,
    e8,
    e16,
    part,
    t8,
    ohh,
    xs,
    wsrc,
    wown,
    wdst,
    we2,
    wn1,
    wn2,
    wenc1,
    wenc2,
    src,
    ordered,
    sbuf,
    r1,
    mid,
    r2,
    hsend,
    hrecv,
    bsend,
    brecv,
    loads,
    s1,
    q1,
    s2,
    q2,
    fs,
    fq,
    bs,
    bq,
):
    gx, gy = lax.axis_index("gx"), lax.axis_index("gy")

    def at_x(step):
        return (lax.rem(gx + (step + nx), nx), gy)

    def at_y(step):
        return (gx, lax.rem(gy + (step + ny), ny))

    barrier = pltpu.get_barrier_semaphore()
    pairs = (
        (flow_hbm, flow),
        (interp_hbm, interp),
        (send_hbm, send_rows),
        (links_hbm, links),
        (halo_hbm, halo),
        (enc_first_hbm, enc_first),
        (enc_second_hbm, enc_second),
        (edge_first_hbm, edge_first),
        (edge_second_hbm, edge_second),
        (node_first_hbm, node_first),
        (node_second_hbm, node_second),
    )
    loading = [
        pltpu.make_async_copy(there, here, loads.at[i]) for i, (there, here) in enumerate(pairs)
    ]
    for copy in loading[:3]:
        copy.start()
    x_steps = sorted(range(1, nx), key=lambda s: -hops(s % 4, 4) - hops(s // 4, nx // 4))
    y_steps = sorted(range(1, ny), key=lambda s: -hops(s, ny))
    for step in x_steps:
        pl.semaphore_signal(barrier, inc=1, device_id=at_x(step), device_id_type=MESH)
    for step in y_steps:
        pl.semaphore_signal(barrier, inc=1, device_id=at_y(step), device_id_type=MESH)
    for copy in loading[3:]:
        copy.start()
    for copy in loading[:3]:
        copy.wait()

    tiles = []
    for e in range(8):
        f = flow[e]
        f = jnp.concatenate([f, f], axis=0)
        tiles.append(jnp.concatenate([f, f, f, f], axis=0))
    flow_high, flow_low = two_terms(jnp.concatenate(tiles, axis=0), BF16)
    main = mm_t(interp[...], flow_high)
    sampled = main[:64] + main[64:] + mm_t(interp[0:64, :], flow_low)
    columns = jnp.concatenate([sampled[:, 32 * e : 32 * e + 32] for e in range(8)], axis=0)
    col_high, col_low = two_terms(columns, BF16)
    table = jnp.concatenate(
        [
            col_high,
            jnp.ones((512, 8), BF16),
            jnp.zeros((512, 88), BF16),
            col_low,
            jnp.zeros((512, 96), BF16),
        ],
        axis=1,
    )
    lane = lax.broadcasted_iota(jnp.int32, (D, D), 1)
    picked = jnp.zeros((D, D), F32)
    ordered[...] = jnp.concatenate([send_rows[0]] * 16, axis=0).T
    slots = jnp.concatenate(
        [ordered[pl.ds(y, nx, stride=ny), :] for y in range(ny)], axis=0
    )
    node_ids = lax.broadcasted_iota(jnp.int32, (D, 512), 1)
    for k in range(SLOTS):
        choose = (slots[:, k : k + 1] == node_ids).astype(F32).astype(BF16)
        both = mm(choose, table)
        mine = ((lane < 32) & (lane // 4 == k)) | (lane == 32 + k)
        picked = picked + jnp.where(mine, both[:, :D] + both[:, D:], 0.0)
    for y in range(ny):
        sbuf[y] = picked[y * nx : y * nx + nx, :]

    pl.semaphore_wait(barrier, nx + ny - 2)

    first = []
    for step in y_steps:
        target = at_y(step)
        copy = pltpu.make_async_remote_copy(
            src_ref=sbuf.at[target[1]],
            dst_ref=r1.at[gy],
            send_sem=s1.at[step - 1],
            recv_sem=q1.at[step - 1],
            device_id=target,
            device_id_type=MESH,
        )
        copy.start()
        first.append(copy)
    r1[gy] = sbuf[gy]
    for copy in loading[3:]:
        copy.wait()

    sub8 = lax.broadcasted_iota(jnp.int32, (D, NODES), 0).astype(jnp.int8)

    def make_oht(k, carry):
        ids = links[pl.ds(k, 1), :]
        where = pl.ds(pl.multiple_of(k * NODES, NODES), NODES)
        for a in range(ROWS // D):
            key = ids - D * a
            key = jnp.where((key >= 0) & (key < D), key, -1).astype(jnp.int8)
            oht[pl.ds(a * D, D), where] = jnp.where(
                key == sub8, jnp.full((), 0.125, F8), jnp.zeros((), F8)
            )
        return carry

    lax.fori_loop(0, SLOTS // 2, make_oht, 0)

    for copy in first:
        copy.wait_recv()
    for x in range(nx):
        mid[x] = r1[:, x, :]
    second = []
    for step in x_steps:
        target = at_x(step)
        copy = pltpu.make_async_remote_copy(
            src_ref=mid.at[target[0]],
            dst_ref=r2.at[gx],
            send_sem=s2.at[step - 1],
            recv_sem=q2.at[step - 1],
            device_id=target,
            device_id_type=MESH,
        )
        copy.start()
        second.append(copy)
    r2[gx] = mid[gx]

    lax.fori_loop(SLOTS // 2, SLOTS, make_oht, 0)

    spread_first = jnp.concatenate([enc_first[...], enc_first[...]], axis=0)
    spread_first = jnp.concatenate([spread_first] * 16, axis=0).T
    enc_high, enc_low = two_terms(jnp.where(lane < 32, spread_first * 0.5, 0.0), BF16)
    wenc1[0:D, 0:D] = enc_high
    wenc1[0:D, D : 2 * D] = enc_high
    wenc1[D : 2 * D, 0:D] = enc_low
    wenc1[D : 2 * D, D : 2 * D] = jnp.zeros((D, D), BF16)
    mark = lax.broadcasted_iota(jnp.int32, (16, 2 * D), 1)
    wenc1[2 * D : 2 * D + 16, :] = ((mark >= 32) & (mark < 40)).astype(F32).astype(BF16)
    wenc2[...] = centred_t(enc_second[...])
    for l in range(LAYERS):
        wown[l] = scaled_t(edge_first[l, 0:D, :], 0.03125)
        wsrc[l] = scaled_t(edge_first[l, D : 2 * D, :], 0.5)
        wdst[l] = scaled_t(edge_first[l, 2 * D : 3 * D, :], 4.0)
        we2[l] = centred_t(edge_second[l])
        wn1[l, :, 0:D] = scaled_t(node_first[l, 0:D, :], 0.5)
        wn1[l, :, D : 2 * D] = scaled_t(node_first[l, D : 2 * D, :], 0.5)
        wn2[l] = centred_t(node_second[l])

    node_rows = lax.broadcasted_iota(jnp.int32, (NODES, D), 0)
    for j, (p, q) in enumerate((((1, 0), (1, 1)), ((0, 0), (0, 1)), ((0, 1), (1, 1)), ((0, 0), (1, 0)))):
        ids = jnp.concatenate([halo[0, p[0], p[1] : p[1] + 1, :], halo[0, q[0], q[1] : q[1] + 1, :]], axis=1)
        ohh[:, D * j : D * j + D] = (ids == node_rows).astype(F32).astype(BF16)

    for copy in first:
        copy.wait_send()
    for copy in second:
        copy.wait_recv()

    sub = lax.broadcasted_iota(jnp.int32, (8, D), 0)
    lane8 = lax.broadcasted_iota(jnp.int32, (8, D), 1)
    keep = ((lane8 < 32) & (lane8 // 4 == sub)) | (lane8 == 32 + sub)
    for x in range(nx):
        for y in range(0, ny, 2):
            rows = jnp.concatenate(
                [
                    jnp.where(keep, jnp.broadcast_to(r2[x, y : y + 1, :], (8, D)), 0.0),
                    jnp.where(keep, jnp.broadcast_to(r2[x, y + 1 : y + 2, :], (8, D)), 0.0),
                ],
                axis=0,
            )
            high, low = two_terms(rows, BF16)
            base = (x * ny + y) * 8
            xs[base : base + 16, 0:D] = high
            xs[base : base + 16, D : 2 * D] = low
    pre = mm_t(wenc1[...], xs[...])
    filled = pre[2 * D : 2 * D + 1, :] > 0.5
    hidden = half_silu(pre[:D] + pre[D : 2 * D]).astype(BF16)
    h = norm_columns(mm(wenc2[...], hidden))
    h = jnp.where(filled, h, 0.0).astype(BF16)
    for copy in second:
        copy.wait_send()

    forward = (at_x(1), at_x(-1), at_y(1), at_y(-1))
    backward = (at_x(-1), at_x(1), at_y(-1), at_y(1))

    for l in range(LAYERS):
        proj = mm(wdst[l], h)
        rounded = proj.astype(BF16)
        copies = []
        for j in range(4):
            if j % 2 == 0:
                border = mm(rounded, ohh[:, D * j : D * j + 2 * D]).astype(BF16)
            hsend[l, j] = border[:, D * (j % 2) : D * (j % 2) + D]
            copy = pltpu.make_async_remote_copy(
                src_ref=hsend.at[l, j],
                dst_ref=hrecv.at[l, j],
                send_sem=fs.at[l, j],
                recv_sem=fq.at[l, j],
                device_id=forward[j],
                device_id_type=MESH,
            )
            copy.start()
            copies.append(copy)
        high, low = two_terms(proj, F8)
        t8[0:D, 0:NODES] = high
        t8[D : 2 * D, 0:NODES] = low
        src[...] = mm(wsrc[l], h)

        def local_step(c, carry):
            where = pl.ds(pl.multiple_of(c * CH, CH), CH)
            got = mm(t8[:, 0:NODES], oht[0:NODES, where])
            u = got[:D] + got[D:] + jnp.concatenate([src[...]] * GROUP, axis=1)
            if l > 0:
                u = u + mm(wown[l], e16[:, where])
            part[c] = u
            return carry

        lax.fori_loop(0, STEPS, local_step, 0, unroll=2)

        def take(j):
            copies[j].wait_recv()
            high, low = two_terms(hrecv[l, j].astype(F32), F8)
            t8[0:D, NODES + D * j : NODES + D * j + D] = high
            t8[D : 2 * D, NODES + D * j : NODES + D * j + D] = low

        take(2)
        take(3)

        def near_step(c, carry):
            where = pl.ds(pl.multiple_of(c * CH, CH), CH)
            got = mm(t8[:, FAR:ROWS], oht[FAR:ROWS, where])
            part[c] = part[c] + got[:D] + got[D:]
            return carry

        lax.fori_loop(0, STEPS, near_step, 0, unroll=2)
        take(0)
        take(1)

        def edge_step(c, carry):
            where = pl.ds(pl.multiple_of(c * CH, CH), CH)
            got = mm(t8[:, NODES:FAR], oht[NODES:FAR, where])
            u = (part[c] + got[:D] + got[D:]).astype(BF16)
            new = norm_columns(mm(we2[l], half_silu(u)), 16.0).astype(BF16)
            if l > 0:
                new = new + e16[:, where]
            if l + 1 < LAYERS:
                e16[:, where] = new
            high = new.astype(F8)
            e8[0:D, where] = high
            e8[D : 2 * D, where] = (new - high.astype(BF16)).astype(F8)
            return carry

        lax.fori_loop(0, STEPS, edge_step, 0, unroll=2)

        sums = mm_t(e8[...], oht[NODES:ROWS, :])
        sums = ((sums[:D] + sums[D:]) * 0.5).astype(BF16)
        back = []
        for j in range(4):
            bsend[l, j] = sums[:, D * j : D * j + D]
            copy = pltpu.make_async_remote_copy(
                src_ref=bsend.at[l, j],
                dst_ref=brecv.at[l, j],
                send_sem=bs.at[l, j],
                recv_sem=bq.at[l, j],
                device_id=backward[j],
                device_id_type=MESH,
            )
            copy.start()
            back.append(copy)
        sums = mm_t(e8[...], oht[0:NODES, :])
        sums = (sums[:D] + sums[D:]) * 0.5
        for j in (2, 0):
            back[j].wait_recv()
            back[j + 1].wait_recv()
            returned = jnp.concatenate([brecv[l, j], brecv[l, j + 1]], axis=1)
            sums = sums + mm_t(returned, ohh[:, D * j : D * j + 2 * D])
        pre = mm(wn1[l], jnp.concatenate([h, sums.astype(BF16)], axis=0))
        new = h.astype(F32) + norm_columns(mm(wn2[l], half_silu(pre).astype(BF16)))
        new = jnp.where(filled, new, 0.0)
        for copy in copies:
            copy.wait_send()
        for copy in back:
            copy.wait_send()
        if l + 1 < LAYERS:
            h = new.astype(BF16)
        else:
            out[...] = new.T.astype(BF16)


def solution(mesh):
    nx, ny = mesh.shape["gx"], mesh.shape["gy"]

    def shards(
        flow_field,
        enc_first,
        enc_second,
        send_rows,
        part_sizes,
        halo_rows,
        neighbours,
        edge_first,
        edge_second,
        node_first,
        node_second,
    ):
        del part_sizes
        vmem = pl.BlockSpec(memory_space=pltpu.VMEM)
        dma = pltpu.SemaphoreType.DMA
        operands = (
            flow_field,
            jnp.asarray(interp_parts()),
            jnp.transpose(send_rows, (0, 2, 1)),
            neighbours,
            halo_rows,
            enc_first,
            enc_second,
            edge_first,
            edge_second,
            node_first,
            node_second,
        )
        return pl.pallas_call(
            functools.partial(kernel, nx, ny),
            out_shape=jax.ShapeDtypeStruct((NODES, D), BF16),
            in_specs=[pl.BlockSpec(memory_space=pltpu.HBM)] * 11,
            out_specs=vmem,
            scratch_shapes=[
                *[pltpu.VMEM(x.shape, x.dtype) for x in operands],
                pltpu.VMEM((ROWS, EDGES), F8),
                pltpu.VMEM((2 * D, EDGES), F8),
                pltpu.VMEM((D, EDGES), BF16),
                pltpu.VMEM((STEPS, D, CH), F32),
                pltpu.VMEM((2 * D, ROWS), F8),
                pltpu.VMEM((NODES, HALO), BF16),
                pltpu.VMEM((NODES, 2 * D), BF16),
                pltpu.VMEM((LAYERS, D, D), BF16),
                pltpu.VMEM((LAYERS, D, D), BF16),
                pltpu.VMEM((LAYERS, D, D), BF16),
                pltpu.VMEM((LAYERS, D, D), BF16),
                pltpu.VMEM((LAYERS, D, 2 * D), BF16),
                pltpu.VMEM((LAYERS, D, D), BF16),
                pltpu.VMEM((2 * D + 16, 2 * D), BF16),
                pltpu.VMEM((D, D), BF16),
                pltpu.VMEM((D, NODES), F32),
                pltpu.VMEM((D, D), jnp.int32),
                pltpu.VMEM((ny, nx, D), F32),
                pltpu.VMEM((ny, nx, D), F32),
                pltpu.VMEM((nx, ny, D), F32),
                pltpu.VMEM((nx, ny, D), F32),
                pltpu.VMEM((LAYERS, 4, D, D), BF16),
                pltpu.VMEM((LAYERS, 4, D, D), BF16),
                pltpu.VMEM((LAYERS, 4, D, D), BF16),
                pltpu.VMEM((LAYERS, 4, D, D), BF16),
                dma((len(operands),)),
                dma((ny - 1,)),
                dma((ny - 1,)),
                dma((nx - 1,)),
                dma((nx - 1,)),
                dma((LAYERS, 4)),
                dma((LAYERS, 4)),
                dma((LAYERS, 4)),
                dma((LAYERS, 4)),
            ],
            compiler_params=pltpu.CompilerParams(
                collective_id=0, has_side_effects=True, vmem_limit_bytes=60 << 20
            ),
        )(*operands)

    in_specs = (
        P(("gx", "gy"), None, None),
        P(),
        P(),
        P(("gx", "gy"), None, None),
        P(("gx", "gy"), None),
        P(("gx", "gy"), None, None, None),
        P(None, ("gx", "gy")),
        P(),
        P(),
        P(),
        P(),
    )
    out_specs = P(("gx", "gy"), None)
    return jax.shard_map(shards, mesh=mesh, in_specs=in_specs, out_specs=out_specs, check_vma=False)
```
